128 devices in a mesh: grp: 4 (over z), sub: 32 (over x, y, core).
Axes of the slice: x: 4, y: 4, z: 4, core: 2. Of those that a mesh axis runs over, the one named last changes fastest.
Arguments:
- three_centre: bfloat16 [64, 8192, 512], P('grp', 'sub'), may hold values from -6 to 6
- pair_blocks: int32 [32, 2], P('sub'), may hold values from 0 to 31, all different within a row
- green_occ: bfloat16 [8192, 1024], P('sub', 'grp'), may hold values from -0.25 to 0.25
- occ_mask: int32 [32, 4], P('sub', 'grp'), may hold values 0 or 1
- green_virt: bfloat16 [1024, 8192], P('grp', 'sub'), may hold values from -0.0625 to 0.0625
- virt_mask: int32 [4, 32], P('grp', 'sub'), may hold values 0 or 1
- owner: int32 [64, 1], replicated, may hold values from 0 to 31; in each aligned block of 64 rows (0 to 63, 64 to 127, ...) at most 3 rows name the same one
Outputs:
- products: float32 [4, 96, 256, 256], P('grp', 'sub')
The draws below stay inside these ranges and needn't reach their ends.
Inputs may be any that keep to these rules, and one draw needn't show every extreme that they name: `pair_blocks`: the 2 partner blocks of a basis block are distinct, and every basis block is some block's partner. No index is the owner of more than 3 RI functions of the slab, and one owns exactly 3.
All inputs are finite; a program needn't handle non-finite values. No bound on the sum of `occ_mask` or of `virt_mask` on one device may be relied on, other than what follows from the above.
Results may differ from the reference program's by a relative error of at most 0.0029.
Values may be sent and summed in bfloat16 or wider, within the bound.
No kernel may reach another device: no remote copies, remote signals or barrier semaphores. Data moves between devices by JAX's collectives and lax.ppermute only.
A program may use at most 128 MiB of HBM per device.

```python
import math
import jax
import jax.numpy as jnp
import numpy as np
from jax import lax

BLK = 256
K = 2
CAP = 3
NBB = 32
NB = 8192
GROUPS = 4
LAM = 1024
NP = 64
N_GRP = 4
N_SUB = 32


def set_ends(result, key, low, top_value):
    spot = [jax.random.randint(jax.random.fold_in(key, axis), (), 0, length) for axis, length in enumerate(result.shape)]
    main_axis = result.shape.index(max(result.shape))
    next_to = spot[:main_axis] + [(spot[main_axis] + 1) % result.shape[main_axis]] + spot[main_axis + 1:]
    return result.at[tuple(spot)].set(low).at[tuple(next_to)].set(top_value)


def block_scale(key, shape, pieces, least, high):
    def one(axis_at, blocks):
        draws = jax.random.uniform(jax.random.fold_in(jax.random.fold_in(key, 6), axis_at), (blocks,), jnp.float32, least / len(pieces), high / len(pieces))
        return jnp.repeat(jnp.exp(draws), shape[axis_at] // blocks).reshape((-1,) + (1,) * (len(shape) - axis_at - 1))

    gain = one(*pieces[0])
    for cut in pieces[1:]:
        gain = gain * one(*cut)
    return gain


def different_ones(own_key, rows, count, top, lift):
    sequence = jax.random.permutation(jax.random.fold_in(own_key, 1), count)
    boost = sequence
    for power in range(3):
        boost = boost * boost // count
    boost = boost * lift // count
    chance = jax.random.randint(jax.random.fold_in(own_key, 2), (rows, count), 0, 4096) + boost
    fixed_rows = jax.random.permutation(jax.random.fold_in(own_key, 3), rows)[jnp.arange(count) % rows]
    chance = jnp.where(jnp.arange(rows)[:, None] == fixed_rows[None, :], 1 << 14, chance)
    priority = chance * count + jnp.arange(count)
    return lax.top_k(priority.astype(jnp.int32), top)[1].astype(jnp.int32)


def deal_out(rng, own, number, rows, count, top, reach, skew):
    order = jax.random.permutation(rng, count)
    heavy_load, ordinary = portions_of(count, rows * top, reach, skew, True), portions_of(count, rows * top, reach, skew, False)
    places = jnp.arange(count)

    def named(lengths, turn):
        used = int((lengths > 0).sum())
        fixed = max(1, used // 4)
        shifted = fixed + (places - fixed + turn * (used - fixed)) % max(1, count - fixed)
        return jnp.zeros((count,), jnp.int32).at[order[jnp.where(places < fixed, places, shifted)]].set(jnp.asarray(lengths, jnp.int32))

    lengths = jnp.where(number % 4 == 0, named(heavy_load, number // 4), named(ordinary, number - number // 4 - 1))
    mixed = jax.random.permutation(jax.random.fold_in(own, 3), count)
    source_of, taker = mixed[0:count // 2 * 2:2], mixed[1:count // 2 * 2:2]
    room = jnp.minimum(lengths[source_of] - 1, reach - lengths[taker]) // 2
    room = jnp.where((source_of == order[0]) | (taker == order[0]) | (lengths[taker] == 0), 0, jnp.maximum(room, 0))
    shifted = jax.random.randint(jax.random.fold_in(own, 4), (count // 2,), 0, 1 << 20) % (room + 1)
    lengths = lengths.at[source_of].add(-shifted).at[taker].add(shifted)
    labels = jnp.searchsorted(jnp.cumsum(lengths), jnp.arange(rows * top), side="right").astype(jnp.int32)
    table = labels.reshape(top, rows).T
    table = table[jax.random.permutation(jax.random.fold_in(own, 1), rows)]
    turn = jax.random.randint(jax.random.fold_in(own, 2), (rows, 1), 0, top)
    return jnp.take_along_axis(table, (jnp.arange(top)[None, :] + turn) % top, axis=1)


def portions_of(count, total, most, lean, full):
    portions = [(1 << 20) // math.isqrt(grade ** lean) + 1 for grade in range(1, count + 1)]
    largest = most if full else min(most, max(-(-total // count), total * portions[0] // sum(portions)))
    least = 1 if total - largest >= count - 1 else 0
    counts, rest = [largest] + [least] * (count - 1), total - largest - least * (count - 1)
    while rest > 0:
        free = [i for i in range(1, count) if counts[i] < largest] or [i for i in range(1, count) if counts[i] < most]
        pool, left = sum([portions[i] for i in free]), rest
        for i in free:
            extra = min(most - counts[i], max(1, left * portions[i] // pool), rest)
            counts[i] = counts[i] + extra
            rest = rest - extra
    return np.array(counts)


def normal_values(rng, extent, spread, limit, split=(), kind=jnp.bfloat16):
    entries = jax.random.normal(rng, extent, jnp.float32) * spread
    if len(split) > 0:
        entries = block_scale(rng, extent, split, -0.22, 0.18) * entries
    return jnp.clip(entries, min=-limit, max=limit).astype(kind)


def setup_inputs(seed: int = 0) -> dict:
    seeds = jax.random.split(jax.random.key(seed), 8)
    three_centre = normal_values(seeds[0], (NP, NB, K * BLK), 1.0, 6.0, ((0, 4), (1, 32)))
    pair_blocks = different_ones(seeds[1], NBB, NBB, K, 0)
    green_occ = normal_values(seeds[2], (NB, LAM), (K * BLK) ** -0.5, 0.25, ((0, 32), (1, 4)))
    occ_mask = set_ends((jax.random.randint(seeds[3], (NBB, GROUPS), 0, 4) < 3).astype(jnp.int32), jax.random.fold_in(seeds[3], 1), 0, 1)
    green_virt = normal_values(seeds[4], (LAM, NB), NB ** -0.5, 0.0625, ((0, 4), (1, 32)))
    virt_mask = set_ends((jax.random.randint(seeds[5], (GROUPS, NBB), 0, 4) < 3).astype(jnp.int32), jax.random.fold_in(seeds[5], 1), 0, 1)
    owner_keys = jax.random.split(jax.random.fold_in(seeds[6], 1), NP // NP)
    owner_turns = jax.random.permutation(jax.random.fold_in(seeds[6], 3), NP // NP)
    owner = jax.vmap(lambda own, number: deal_out(jax.random.fold_in(seeds[6], 2), own, number, NP, N_SUB, 1, CAP, 2))(owner_keys, owner_turns).reshape((NP, 1))
    return {"three_centre": three_centre, "pair_blocks": pair_blocks, "green_occ": green_occ, "occ_mask": occ_mask, "green_virt": green_virt, "virt_mask": virt_mask, "owner": owner}


def reference(three_centre, pair_blocks, green_occ, occ_mask, green_virt, virt_mask, owner):
    occ_full = jnp.repeat(jnp.repeat(occ_mask, BLK, axis=0), BLK, axis=1)
    go_masked = green_occ * occ_full.astype(green_occ.dtype)
    virt_full = jnp.repeat(jnp.repeat(virt_mask, BLK, axis=0), BLK, axis=1)
    gv_masked = green_virt * virt_full.astype(green_virt.dtype)
    picked = go_masked.reshape(NBB, BLK, LAM)[pair_blocks]
    picked = picked.reshape(NBB, K * BLK, LAM)
    owner_flat = owner[:, 0].astype(jnp.int32)
    numbers = jnp.arange(NP).astype(jnp.int32)
    earlier = (owner_flat[None, :] == owner_flat[:, None]) & (numbers[None, :] < numbers[:, None])
    position = jnp.sum(earlier.astype(jnp.int32), axis=1).astype(jnp.int32)
    slots = owner_flat * CAP + position

    def group_columns(group):
        start = (group * BLK).astype(jnp.int32)
        return lax.dynamic_slice_in_dim(picked, start, BLK, 2).astype(jnp.float32)

    def one_function(index):
        rows = three_centre[index].reshape(NBB, BLK, K * BLK).astype(jnp.float32)

        def one_group(group):
            start = (group * BLK).astype(jnp.int32)
            columns = group_columns(group)
            half = jnp.einsum("bmk,bkl->bml", rows, columns).astype(jnp.bfloat16).reshape(NB, BLK)
            virt_rows = lax.dynamic_slice_in_dim(gv_masked, start, BLK, 0)
            return jnp.dot(virt_rows, half, preferred_element_type=jnp.float32)

        return lax.map(one_group, jnp.arange(N_GRP).astype(jnp.int32))

    results = lax.map(one_function, numbers)
    products = jnp.zeros((N_GRP, N_SUB * CAP, BLK, BLK), jnp.float32)
    products = products.at[:, slots].set(jnp.transpose(results, (1, 0, 2, 3)).astype(jnp.float32))
    return products
```

```python
import functools

import jax
import jax.numpy as jnp
from jax import lax
from jax.experimental import pallas as pl
from jax.experimental.pallas import tpu as pltpu
from jax.sharding import PartitionSpec as P

CAP = 3
AXES = ("grp", "sub")
BF = jnp.bfloat16
F32 = jnp.float32
SWAP = (0, 2, 1, 3)


def pairs(target):
    out = []
    for z in range(4):
        for x in range(4):
            for y in range(4):
                for c in range(2):
                    tz, tx, ty, tc = target(z, x, y, c)
                    out.append((z * 32 + (x * 4 + y) * 2 + c, tz * 32 + (tx * 4 + ty) * 2 + tc))
    return out


def first(c):
    return 1 if c == 0 else 3


CORE = pairs(lambda z, x, y, c: (z, x, y, 1 - c))
Z1 = pairs(lambda z, x, y, c: (z ^ first(c), x, y, c))
Z2 = pairs(lambda z, x, y, c: (z ^ first(1 - c), x, y, c))
X_A = pairs(lambda z, x, y, c: (z, x ^ first(c), y, c))
X_B = pairs(lambda z, x, y, c: (z, x ^ first(1 - c), y, c))
Y_A = pairs(lambda z, x, y, c: (z, x, y ^ first(c), c))
Y_B = pairs(lambda z, x, y, c: (z, x, y ^ first(1 - c), c))


def on(axis0, e):
    def target(z, x, y, c):
        return (z, x ^ e, y, c) if (c == axis0) else (z, x, y ^ e, c)

    return pairs(target)


def move(value, permutation):
    return lax.ppermute(value, AXES, permutation)


def place(d, e):
    return jnp.where(d == 0, 0, jnp.where(d == 2, 3, jnp.where(d == e, 1, 2)))


def ring_order(q, e):
    return [q ^ 2, q ^ e, q ^ (4 - e), q]


def products_body(sc, t_own, t_oth, go_own, go_oth, gv_own, gv_oth, send, keep, gvp, half):
    @pl.when(pl.program_id(0) == 0)
    def _():
        for k in range(16):
            rows = pl.ds(pl.multiple_of(sc[1 + k] * 16, 16), 16)
            for g in range(4):
                gvp[g, k * 16 : (k + 1) * 16, 0:256] = gv_own[g, rows, :]
                gvp[g, k * 16 : (k + 1) * 16, 256:512] = gv_oth[SWAP[g], rows, :]

    for g in range(4):
        half[0:256, :] = jnp.dot(t_own[0], go_own[g], preferred_element_type=F32).astype(BF)
        half[256:512, :] = jnp.dot(t_oth[0], go_oth[SWAP[g]], preferred_element_type=F32).astype(BF)
        out = jnp.dot(gvp[g], half[...], preferred_element_type=F32)
        send[0, g] = out[0:128].astype(BF)
        keep[0, g] = out[128:256]


def products_of(part, scalars, t_own, t_oth, go_own, go_oth, gv_own, gv_oth):
    whole = lambda shape: pl.BlockSpec(shape, lambda p, sc: (0,) * len(shape))
    return pl.pallas_call(
        products_body,
        grid_spec=pltpu.PrefetchScalarGridSpec(
            num_scalar_prefetch=1,
            grid=(4,),
            in_specs=[
                pl.BlockSpec((1, 256, 512), lambda p, sc: (sc[0] * 8 + part * 4 + p, 0, 0)),
                pl.BlockSpec((1, 256, 512), lambda p, sc: (part * 4 + p, 0, 0)),
                whole((4, 512, 256)),
                whole((4, 512, 256)),
                whole((4, 256, 256)),
                whole((4, 256, 256)),
            ],
            out_specs=[
                pl.BlockSpec((1, 4, 128, 256), lambda p, sc: (p, 0, 0, 0)),
                pl.BlockSpec((1, 4, 128, 256), lambda p, sc: (p, 0, 0, 0)),
            ],
            scratch_shapes=[pltpu.VMEM((4, 256, 512), BF), pltpu.VMEM((512, 256), BF)],
        ),
        out_shape=[
            jax.ShapeDtypeStruct((4, 4, 128, 256), BF),
            jax.ShapeDtypeStruct((4, 4, 128, 256), F32),
        ],
        compiler_params=pltpu.CompilerParams(vmem_limit_bytes=32 * 1024 * 1024),
        cost_estimate=pl.CostEstimate(flops=3_300_000_000, bytes_accessed=12_000_000, transcendentals=0),
    )(scalars, t_own, t_oth, go_own, go_oth, gv_own, gv_oth)


def slots_body(sc, mine, other, out):
    for s in range(32 * CAP):
        at = sc[s]

        @pl.when(at < 0)
        def _():
            out[s] = jnp.zeros_like(out[s])

        @pl.when((at >= 0) & (at < 32))
        def _():
            out[s] = mine[jnp.clip(at, 0, 31)]

        @pl.when(at >= 32)
        def _():
            out[s] = other[jnp.clip(at - 32, 0, 31)]


def fill_slots(source, mine, other):
    whole = lambda shape: pl.BlockSpec(shape, lambda i, sc: (0,) * len(shape))
    return pl.pallas_call(
        slots_body,
        grid_spec=pltpu.PrefetchScalarGridSpec(
            num_scalar_prefetch=1,
            grid=(1,),
            in_specs=[whole((32, 8, 256)), whole((32, 8, 256))],
            out_specs=whole((32 * CAP, 8, 256)),
        ),
        out_shape=jax.ShapeDtypeStruct((32 * CAP, 8, 256), F32),
    )(source, mine, other)


def reduce_steps(send, keep, steps):
    got = []
    begin = 0
    for number, step in enumerate(steps):
        if number:
            size = 128 >> number
            total = keep[:, :, begin : begin + size]
            offset = begin
            for level, part in enumerate(got):
                total = total + part[:, :, offset : offset + size].astype(F32)
                offset -= 64 >> level
            send = total.astype(BF)
            begin += size
        got.append(move(send, step))
    total = keep[:, :, begin : begin + 16]
    offset = begin
    for level, part in enumerate(got):
        total = total + part[:, :, offset : offset + 16].astype(F32)
        offset -= 64 >> level
    return total


def per_device(three_centre, pair_blocks, green_occ, occ_mask, green_virt, virt_mask, owner):
    z = lax.axis_index("grp")
    sub = lax.axis_index("sub")
    x, y, c = sub // 8, (sub // 2) % 4, sub % 2
    e = 1 + 2 * c

    t_oth = move(lax.dynamic_slice_in_dim(three_centre, (1 - c) * 8, 8, 0), CORE)
    pair_oth = move(pair_blocks, CORE)

    gv = green_virt * virt_mask[0, 0].astype(BF)
    gv1 = move(gv, Z1)
    gv = jnp.stack([gv, gv1])
    gv2 = move(gv, Z2)
    gv = jnp.concatenate([gv, gv2])
    gv_oth = move(gv, CORE)

    go = green_occ * occ_mask[0, 0].astype(BF)
    set1 = jnp.stack([go, move(go, on(0, 1))])
    set2 = move(set1, on(0, 3))
    a1 = jnp.stack([set1, move(set1, on(1, 1))])
    b1 = jnp.stack([set2, move(set2, on(1, 3))])
    a2 = jnp.concatenate([a1, move(a1, on(1, 3))])
    b2 = jnp.concatenate([b1, move(b1, on(1, 1))])

    def block_from(target):
        tx, ty = target // 8, (target // 2) % 4
        d1 = jnp.where(c == 0, x ^ tx, y ^ ty)
        d2 = jnp.where(c == 0, y ^ ty, x ^ tx)
        p1 = place(d1, 1)
        in_a = lax.dynamic_slice(a2, (place(d2, 1), p1 % 2, 0, 0), (1, 1, 256, 256))
        in_b = lax.dynamic_slice(b2, (place(d2, 3), p1 % 2, 0, 0), (1, 1, 256, 256))
        return jnp.where(p1 < 2, in_a, in_b).reshape(256, 256)

    for_oth = move(jnp.concatenate([block_from(pair_oth[0, k]) for k in range(2)]), CORE)
    go = jnp.concatenate(
        [
            jnp.where(
                pair_blocks[0, k] % 2 == c,
                block_from(pair_blocks[0, k]),
                for_oth[k * 256 : (k + 1) * 256],
            )
            for k in range(2)
        ]
    )
    go = jnp.stack([go, move(go, Z1)])
    go = jnp.concatenate([go, move(go, Z2)])
    go_oth = move(go, CORE)

    order_x, order_y = ring_order(x, e), ring_order(y, e)
    strips_a = [i * 4 + j for i in order_x for j in order_y]
    strips_b = [i * 4 + j for j in order_y for i in order_x]
    operands = (three_centre, t_oth, go, go_oth, gv, gv_oth)
    send_a, keep_a = products_of(0, jnp.stack([c] + strips_a).astype(jnp.int32), *operands)
    send_b, keep_b = products_of(1, jnp.stack([c] + strips_b).astype(jnp.int32), *operands)
    sum_a = reduce_steps(send_a, keep_a, (X_A, X_B, Y_A, Y_B))
    sum_b = reduce_steps(send_b, keep_b, (Y_A, Y_B, X_A, X_B))
    total = jnp.concatenate([sum_a, sum_b]).transpose(1, 0, 2, 3)

    got1 = move(jnp.stack([total[1], total[3]]), Z1)
    got2 = move(jnp.stack([total[2], got1[1]]), Z2)
    whole = jnp.concatenate([total[0:1], got1[0:1], got2])

    mine = lax.dynamic_slice_in_dim(whole, c * 8, 8, 2)
    other = move(lax.dynamic_slice_in_dim(whole, (1 - c) * 8, 8, 2), CORE)

    owner_flat = owner[:, 0]
    slab = owner_flat.shape[0]
    numbers = jnp.arange(slab, dtype=jnp.int32)
    earlier = (owner_flat[None, :] == owner_flat[:, None]) & (numbers[None, :] < numbers[:, None])
    position = jnp.sum(earlier.astype(jnp.int32), axis=1)
    slots = owner_flat * CAP + position
    d = (numbers // 16) ^ z
    core = (numbers // 8) % 2
    at = jnp.where(core == c, 0, 32) + place(d, 1 + 2 * core) * 8 + numbers % 8
    match = slots[None, :] == jnp.arange(32 * CAP, dtype=jnp.int32)[:, None]
    source = jnp.max(jnp.where(match, at[None, :], -1), axis=1)
    outgoing = fill_slots(source, mine.reshape(32, 8, 256), other.reshape(32, 8, 256))
    arrived = lax.all_to_all(
        outgoing.reshape(32, CAP, 8, 256), "sub", split_axis=0, concat_axis=0, tiled=True
    )
    return arrived.transpose(1, 0, 2, 3).reshape(1, CAP, 256, 256)


def solution(mesh):
    in_specs = (
        P("grp", "sub", None),
        P("sub", None),
        P("sub", "grp"),
        P("sub", "grp"),
        P("grp", "sub"),
        P("grp", "sub"),
        P(),
    )
    out_specs = P("grp", "sub", None, None)
    return jax.shard_map(
        per_device, mesh=mesh, in_specs=in_specs, out_specs=out_specs, check_vma=False
    )
```

```python
import jax
import jax.numpy as jnp
from jax import lax
from jax.experimental import pallas as pl
from jax.experimental.pallas import tpu as pltpu
from jax.sharding import PartitionSpec as P

CAP = 3
AXES = ("grp", "sub")
BF = jnp.bfloat16
F32 = jnp.float32
STACK = 4


def pairs(target):
    out = []
    for z in range(4):
        for x in range(4):
            for y in range(4):
                for c in range(2):
                    tz, tx, ty, tc = target(z, x, y, c)
                    to = (tz % 4) * 32 + ((tx % 4) * 4 + ty % 4) * 2 + tc
                    out.append((z * 32 + (x * 4 + y) * 2 + c, to))
    return out


def along(number, d):
    def target(z, x, y, c):
        return (z, x + d, y, c) if c == number else (z, x, y + d, c)

    return pairs(target)


CORE = pairs(lambda z, x, y, c: (z, x, y, 1 - c))
FIRST = [along(0, d) for d in range(4)]
SECOND = [along(1, d) for d in range(4)]
DEPTH = [pairs(lambda z, x, y, c, d=d: (z + d, x, y, c)) for d in range(4)]


def move(value, permutation):
    return lax.ppermute(value, AXES, permutation)


def whole(shape):
    return pl.BlockSpec(shape, lambda *_: (0,) * len(shape))


def pick_body(sc, set0, set1, set2, set3, out, sem):
    c = sc[0]
    for k in range(4):
        block = sc[3 + k]
        tx, ty, tc = block // 8, (block // 2) % 4, block % 2
        t1 = jnp.where(c == 0, tx, ty)
        t2 = jnp.where(c == 0, ty, tx)
        at = ((sc[1] - t1 + 4) % 4) * 2 + tc
        far = (sc[2] - t2 + 4) % 4
        for e, source in enumerate((set0, set1, set2, set3)):

            @pl.when(far == e)
            def _(source=source):
                pltpu.make_async_copy(source.at[at], out.at[k], sem.at[k]).start()

    for k in range(4):
        pltpu.make_async_copy(set0.at[0], out.at[k], sem.at[k]).wait()


def pick(scalars, *sets):
    return pl.pallas_call(
        pick_body,
        grid_spec=pltpu.PrefetchScalarGridSpec(
            num_scalar_prefetch=1,
            grid=(1,),
            in_specs=[pl.BlockSpec(memory_space=pl.ANY)] * 4,
            out_specs=pl.BlockSpec(memory_space=pl.ANY),
            scratch_shapes=[pltpu.SemaphoreType.DMA((4,))],
        ),
        out_shape=jax.ShapeDtypeStruct((4, 128, 256), BF),
        cost_estimate=pl.CostEstimate(flops=0, bytes_accessed=600_000, transcendentals=0),
    )(scalars, *sets)


def order_body(sc, own, oth, out):
    for k in range(16):
        rows = pl.ds(pl.multiple_of(sc[k] * 16, 16), 16)
        for g in range(4):
            out[g, k * 16 : (k + 1) * 16, 0:256] = own[g, rows, :]
            out[g, k * 16 : (k + 1) * 16, 256:512] = oth[g, rows, :]


def order_rows(strips, own, oth):
    return pl.pallas_call(
        order_body,
        grid_spec=pltpu.PrefetchScalarGridSpec(
            num_scalar_prefetch=1,
            grid=(1,),
            in_specs=[whole((4, 256, 256))] * 2,
            out_specs=whole((4, 256, 512)),
        ),
        out_shape=jax.ShapeDtypeStruct((4, 256, 512), BF),
        cost_estimate=pl.CostEstimate(flops=0, bytes_accessed=2_000_000, transcendentals=0),
    )(strips, own, oth)


def products_body(sc, t_own, t_oth, go, gv, send1, send2, send3, keep):
    c = sc[0]
    count = go.shape[0] // 2
    for r in range(count):
        half_own = jnp.dot(
            t_own[...].reshape(STACK * 256, 512), go[2 * r + c], preferred_element_type=F32
        ).astype(BF)
        half_oth = jnp.dot(
            t_oth[...].reshape(STACK * 256, 512), go[2 * r + 1 - c], preferred_element_type=F32
        ).astype(BF)
        for p in range(STACK):
            rows = slice(p * 256, (p + 1) * 256)
            out = jnp.dot(gv[r, :, 0:256], half_own[rows], preferred_element_type=F32)
            out += jnp.dot(gv[r, :, 256:512], half_oth[rows], preferred_element_type=F32)
            send1[p, r] = out[0:64].astype(BF)
            send2[p, r] = out[64:128].astype(BF)
            send3[p, r] = out[128:192].astype(BF)
            keep[p, r] = out[192:256]


def products_of(core, t_own, t_oth, go, gv):
    count = gv.shape[0]
    block = pl.BlockSpec((STACK, count, 64, 256), lambda p, sc: (p, 0, 0, 0))
    shape = (8, count, 64, 256)
    return pl.pallas_call(
        products_body,
        grid_spec=pltpu.PrefetchScalarGridSpec(
            num_scalar_prefetch=1,
            grid=(8 // STACK,),
            in_specs=[
                pl.BlockSpec((STACK, 256, 512), lambda p, sc: (sc[0] * (8 // STACK) + p, 0, 0)),
                pl.BlockSpec((STACK, 256, 512), lambda p, sc: (p, 0, 0)),
                whole((2 * count, 512, 256)),
                whole((count, 256, 512)),
            ],
            out_specs=[block] * 4,
        ),
        out_shape=[jax.ShapeDtypeStruct(shape, BF)] * 3 + [jax.ShapeDtypeStruct(shape, F32)],
        compiler_params=pltpu.CompilerParams(vmem_limit_bytes=40 * 1024 * 1024),
        cost_estimate=pl.CostEstimate(
            flops=1_600_000_000 * count, bytes_accessed=4_000_000 * count, transcendentals=0
        ),
    )(core, t_own, t_oth, go, gv)


def slots_body(sc, pieces, out):
    for s in range(32 * CAP):
        out[s] = pieces[sc[s]]


def fill_slots(source, pieces):
    return pl.pallas_call(
        slots_body,
        grid_spec=pltpu.PrefetchScalarGridSpec(
            num_scalar_prefetch=1,
            grid=(1,),
            in_specs=[whole((65, 16, 128))],
            out_specs=whole((32 * CAP, 16, 128)),
        ),
        out_shape=jax.ShapeDtypeStruct((32 * CAP, 16, 128), BF),
    )(source, pieces)


def per_device(three_centre, pair_blocks, green_occ, occ_mask, green_virt, virt_mask, owner):
    z = lax.axis_index("grp")
    sub = lax.axis_index("sub")
    x, y, c = sub // 8, (sub // 2) % 4, sub % 2
    q1, q2 = jnp.where(c == 0, x, y), jnp.where(c == 0, y, x)

    def by_core(mine, other):
        return jnp.where(c == 0, jnp.stack([mine, other]), jnp.stack([other, mine]))

    go = green_occ * occ_mask[0, 0].astype(BF)
    go = by_core(
        lax.dynamic_slice_in_dim(go, c * 128, 128, 0),
        move(lax.dynamic_slice_in_dim(go, (1 - c) * 128, 128, 0), CORE),
    )
    near = jnp.concatenate([go] + [move(go, FIRST[d]) for d in (1, 2, 3)])
    sets = [near] + [move(near, SECOND[e]) for e in (1, 2, 3)]

    t_oth = move(lax.dynamic_slice_in_dim(three_centre, (1 - c) * 8, 8, 0), CORE)

    gv = green_virt * virt_mask[0, 0].astype(BF)
    gv = jnp.stack([gv] + [move(gv, DEPTH[r]) for r in (1, 2, 3)])
    strips = [
        jnp.where(c == 0, s1 * 4 + s2, s2 * 4 + s1)
        for s1 in [(q1 + d) % 4 for d in (1, 2, 3, 0)]
        for s2 in [(q2 + e) % 4 for e in range(4)]
    ]
    gv = order_rows(jnp.stack(strips).astype(jnp.int32), gv, move(gv, CORE))

    partners = by_core(pair_blocks[0], move(pair_blocks, CORE)[0]).reshape(4)
    places = jnp.concatenate([jnp.stack([c, q1, q2]), partners]).astype(jnp.int32)
    picked = pick(places, *sets)
    picks = [picked] + [move(picked, DEPTH[r]) for r in (1, 2, 3)]

    def rows_of(part):
        halves = by_core(part, move(part, CORE))
        return halves.transpose(1, 0, 2, 3).reshape(2, 512, 256)

    core = c.reshape(1).astype(jnp.int32)
    lists = []
    for begin, end in ((0, 1), (1, 4)):
        lists.append(
            products_of(
                core,
                three_centre,
                t_oth,
                jnp.concatenate([rows_of(picks[r]) for r in range(begin, end)]),
                gv[begin:end],
            )
        )

    sums = []
    for send1, send2, send3, keep in lists:
        total = keep
        for d, send in ((1, send1), (2, send2), (3, send3)):
            total = total + move(send, FIRST[d]).astype(F32)
        sums.append(total)

    def strip(e):
        return jnp.concatenate([t[:, :, e * 16 : (e + 1) * 16] for t in sums], axis=1)

    total = strip(0)
    for e in (1, 2, 3):
        total = total + move(strip(e).astype(BF), SECOND[e]).astype(F32)
    total = total.astype(BF)

    rows = jnp.stack([total[:, 0]] + [move(total[:, r], DEPTH[4 - r]) for r in (1, 2, 3)])
    mine = lax.dynamic_slice_in_dim(rows, c * 128, 128, 3)
    other = move(lax.dynamic_slice_in_dim(rows, (1 - c) * 128, 128, 3), CORE)
    pieces = jnp.concatenate(
        [mine.reshape(32, 16, 128), other.reshape(32, 16, 128), jnp.zeros((1, 16, 128), BF)]
    )

    owner_flat = owner[:, 0]
    slab = owner_flat.shape[0]
    numbers = jnp.arange(slab, dtype=jnp.int32)
    earlier = (owner_flat[None, :] == owner_flat[:, None]) & (numbers[None, :] < numbers[:, None])
    position = jnp.sum(earlier.astype(jnp.int32), axis=1)
    slots = owner_flat * CAP + position
    distance = (numbers // 16 - z + 4) % 4
    at = jnp.where((numbers // 8) % 2 == c, 0, 32) + distance * 8 + numbers % 8
    match = slots[None, :] == jnp.arange(32 * CAP, dtype=jnp.int32)[:, None]
    source = jnp.min(jnp.where(match, at[None, :], 64), axis=1)
    outgoing = fill_slots(source, pieces)
    arrived = lax.all_to_all(
        outgoing.reshape(32, CAP, 16, 128), "sub", split_axis=0, concat_axis=0, tiled=True
    )
    arrived = arrived.reshape(16, 2, CAP, 16, 128).transpose(2, 0, 3, 1, 4)
    return arrived.reshape(1, CAP, 256, 256).astype(F32)


def solution(mesh):
    in_specs = (
        P("grp", "sub", None),
        P("sub", None),
        P("sub", "grp"),
        P("sub", "grp"),
        P("grp", "sub"),
        P("grp", "sub"),
        P(),
    )
    out_specs = P("grp", "sub", None, None)
    return jax.shard_map(
        per_device, mesh=mesh, in_specs=in_specs, out_specs=out_specs, check_vma=False
    )
```

```python
import jax
import jax.numpy as jnp
from jax import lax
from jax.experimental import pallas as pl
from jax.experimental.pallas import tpu as pltpu
from jax.sharding import PartitionSpec as P

CAP = 3
AXES = ("grp", "sub")
BF = jnp.bfloat16
F32 = jnp.float32
MIB = 1024 * 1024
STACK = 4


def pairs(target):
    out = []
    for z in range(4):
        for x in range(4):
            for y in range(4):
                for c in range(2):
                    tz, tx, ty, tc = target(z, x, y, c)
                    to = (tz % 4) * 32 + ((tx % 4) * 4 + ty % 4) * 2 + tc
                    out.append((z * 32 + (x * 4 + y) * 2 + c, to))
    return out


def along(number, d):
    def target(z, x, y, c):
        return (z, x + d, y, c) if c == number else (z, x, y + d, c)

    return pairs(target)


CORE = pairs(lambda z, x, y, c: (z, x, y, 1 - c))
FIRST = [along(0, d) for d in range(4)]
SECOND = [along(1, d) for d in range(4)]
DEPTH = [pairs(lambda z, x, y, c, d=d: (z + d, x, y, c)) for d in range(4)]


def move(value, permutation):
    return lax.ppermute(value, AXES, permutation)


def tie(*values):
    return lax.optimization_barrier(values)


def whole(shape):
    return pl.BlockSpec(shape, lambda *_: (0,) * len(shape))


def pick_body(sc, set0, set1, set2, set3, out, sem):
    c = sc[0]
    for k in range(4):
        block = sc[3 + k]
        tx, ty, tc = block // 8, (block // 2) % 4, block % 2
        t1 = jnp.where(c == 0, tx, ty)
        t2 = jnp.where(c == 0, ty, tx)
        at = ((sc[1] - t1 + 4) % 4) * 2 + tc
        far = (sc[2] - t2 + 4) % 4
        for e, source in enumerate((set0, set1, set2, set3)):

            @pl.when(far == e)
            def _(source=source):
                pltpu.make_async_copy(source.at[at], out.at[k], sem.at[k]).start()

    for k in range(4):
        pltpu.make_async_copy(set0.at[0], out.at[k], sem.at[k]).wait()


def pick(scalars, *sets):
    return pl.pallas_call(
        pick_body,
        grid_spec=pltpu.PrefetchScalarGridSpec(
            num_scalar_prefetch=1,
            grid=(1,),
            in_specs=[pl.BlockSpec(memory_space=pl.ANY)] * 4,
            out_specs=whole((4, 128, 256)),
            scratch_shapes=[pltpu.SemaphoreType.DMA((4,))],
        ),
        out_shape=jax.ShapeDtypeStruct((4, 128, 256), BF),
        compiler_params=pltpu.CompilerParams(vmem_limit_bytes=4 * MIB),
        cost_estimate=pl.CostEstimate(flops=0, bytes_accessed=600_000, transcendentals=0),
    )(scalars, *sets)


def order_body(sc, own, oth, out):
    for k in range(16):
        rows = pl.ds(pl.multiple_of(sc[k] * 16, 16), 16)
        to = slice(k * 16, (k + 1) * 16)
        for r in range(out.shape[0]):
            out[r, to, 0:256] = own[r, rows, :]
            out[r, to, 256:512] = oth[r, rows, :]


def order_rows(strips, own, oth):
    count = own.shape[0]
    return pl.pallas_call(
        order_body,
        grid_spec=pltpu.PrefetchScalarGridSpec(
            num_scalar_prefetch=1,
            grid=(1,),
            in_specs=[whole((count, 256, 256))] * 2,
            out_specs=whole((count, 256, 512)),
        ),
        out_shape=jax.ShapeDtypeStruct((count, 256, 512), BF),
        compiler_params=pltpu.CompilerParams(vmem_limit_bytes=8 * MIB),
        cost_estimate=pl.CostEstimate(flops=0, bytes_accessed=500_000 * count, transcendentals=0),
    )(strips, own, oth)


def products_body(sc, t_own, t_oth, gv, *refs):
    halves, (send1, send2, send3, keep, go) = refs[:-5], refs[-5:]
    count = len(halves) // 2
    c = sc[0]

    @pl.when(pl.program_id(0) == 0)
    def _():
        for r in range(count):
            for n, half in enumerate((c, 1 - c)):
                for k in range(4):
                    rows = pl.ds(pl.multiple_of((k % 2) * 256 + half * 128, 128), 128)
                    go[2 * r + k // 2, rows, :] = halves[2 * r + n][k]

    for r in range(count):
        half_own = jnp.dot(
            t_own[...].reshape(STACK * 256, 512), go[2 * r + c], preferred_element_type=F32
        ).astype(BF)
        half_oth = jnp.dot(
            t_oth[...].reshape(STACK * 256, 512), go[2 * r + 1 - c], preferred_element_type=F32
        ).astype(BF)
        for p in range(STACK):
            rows = slice(p * 256, (p + 1) * 256)
            out = jnp.dot(gv[r, :, 0:256], half_own[rows], preferred_element_type=F32)
            out += jnp.dot(gv[r, :, 256:512], half_oth[rows], preferred_element_type=F32)
            send1[p, r] = out[0:64].astype(BF)
            send2[p, r] = out[64:128].astype(BF)
            send3[p, r] = out[128:192].astype(BF)
            keep[p, r] = out[192:256]


def products_of(core, t_own, t_oth, gv, halves):
    count = gv.shape[0]
    block = pl.BlockSpec((STACK, count, 64, 256), lambda p, sc: (p, 0, 0, 0))
    shape = (8, count, 64, 256)
    functions = pl.BlockSpec((STACK, 256, 512), lambda p, sc: (sc[0] * (8 // STACK) + p, 0, 0))
    return pl.pallas_call(
        products_body,
        grid_spec=pltpu.PrefetchScalarGridSpec(
            num_scalar_prefetch=1,
            grid=(8 // STACK,),
            in_specs=[functions] * 2
            + [whole((count, 256, 512))]
            + [whole((4, 128, 256))] * (2 * count),
            out_specs=[block] * 4,
            scratch_shapes=[pltpu.VMEM((2 * count, 512, 256), BF)],
        ),
        out_shape=[jax.ShapeDtypeStruct(shape, BF)] * 3 + [jax.ShapeDtypeStruct(shape, F32)],
        compiler_params=pltpu.CompilerParams(vmem_limit_bytes=(12 + 4 * count) * MIB),
        cost_estimate=pl.CostEstimate(
            flops=1_600_000_000 * count, bytes_accessed=4_000_000 * count, transcendentals=0
        ),
    )(core, pltpu.with_memory_space_constraint(t_own, pltpu.HBM), t_oth, gv, *halves)


def slots_body(sc, pieces, out):
    for s in range(32 * CAP):
        out[s] = pieces[sc[s]]


def fill_slots(source, pieces):
    return pl.pallas_call(
        slots_body,
        grid_spec=pltpu.PrefetchScalarGridSpec(
            num_scalar_prefetch=1,
            grid=(1,),
            in_specs=[whole((65, 16, 128))],
            out_specs=whole((32 * CAP, 16, 128)),
        ),
        out_shape=jax.ShapeDtypeStruct((32 * CAP, 16, 128), BF),
        compiler_params=pltpu.CompilerParams(vmem_limit_bytes=4 * MIB),
    )(source, pieces)


def per_device(three_centre, pair_blocks, green_occ, occ_mask, green_virt, virt_mask, owner):
    z = lax.axis_index("grp")
    sub = lax.axis_index("sub")
    x, y, c = sub // 8, (sub // 2) % 4, sub % 2
    q1, q2 = jnp.where(c == 0, x, y), jnp.where(c == 0, y, x)

    def by_core(mine, other):
        return jnp.where(c == 0, jnp.stack([mine, other]), jnp.stack([other, mine]))

    go = green_occ * occ_mask[0, 0].astype(BF)
    go = by_core(
        lax.dynamic_slice_in_dim(go, c * 128, 128, 0),
        move(lax.dynamic_slice_in_dim(go, (1 - c) * 128, 128, 0), CORE),
    )
    go, theirs = tie(go, three_centre)
    t_oth = move(theirs, CORE)

    near = jnp.concatenate([go] + [move(go, FIRST[d]) for d in (1, 2, 3)])
    gv = green_virt * virt_mask[0, 0].astype(BF)
    near, gv = tie(near, gv)
    sets = [near] + [move(near, SECOND[e]) for e in (1, 2, 3)]
    gv_far = jnp.stack([move(gv, DEPTH[r]) for r in (1, 2, 3)])
    gv = gv.reshape(1, 256, 256)
    strips = jnp.stack(
        [
            jnp.where(c == 0, s1 * 4 + s2, s2 * 4 + s1)
            for s1 in [(q1 + d) % 4 for d in (1, 2, 3, 0)]
            for s2 in [(q2 + e) % 4 for e in range(4)]
        ]
    ).astype(jnp.int32)
    gv_near = order_rows(strips, gv, move(gv, CORE))

    partners = by_core(pair_blocks[0], move(pair_blocks, CORE)[0]).reshape(4)
    places = jnp.concatenate([jnp.stack([c, q1, q2]), partners]).astype(jnp.int32)
    places, gv_near, gv_far, *sets = tie(places, gv_near, gv_far, *sets)
    picked = pick(places, *sets)
    arriving = [move(picked, DEPTH[r]) for r in (1, 2, 3)]
    gv_far = order_rows(strips, gv_far, move(gv_far, CORE))

    core = c.reshape(1).astype(jnp.int32)
    sends0 = products_of(core, three_centre, t_oth, gv_near, (picked, move(picked, CORE)))
    got0 = [move(sends0[d - 1], FIRST[d]) for d in (1, 2, 3)]
    *got0, a1, a2, a3 = tie(*got0, *arriving)
    halves = [h for a in (a1, a2, a3) for h in (a, move(a, CORE))]
    sends1 = products_of(core, three_centre, t_oth, gv_far, halves)

    def sum_of(sends, got):
        total = sends[3]
        for part in got:
            total = total + part.astype(F32)
        return total

    got1 = [move(sends1[d - 1], FIRST[d]) for d in (1, 2, 3)]
    sums = [sum_of(sends0, got0), sum_of(sends1, got1)]

    def strip(e):
        return jnp.concatenate([t[:, :, e * 16 : (e + 1) * 16] for t in sums], axis=1)

    total = strip(0)
    for e in (1, 2, 3):
        total = total + move(strip(e).astype(BF), SECOND[e]).astype(F32)
    total = total.astype(BF)

    rows = jnp.stack([total[:, 0]] + [move(total[:, r], DEPTH[4 - r]) for r in (1, 2, 3)])
    mine = lax.dynamic_slice_in_dim(rows, c * 128, 128, 3)
    other = move(lax.dynamic_slice_in_dim(rows, (1 - c) * 128, 128, 3), CORE)
    pieces = jnp.concatenate(
        [mine.reshape(32, 16, 128), other.reshape(32, 16, 128), jnp.zeros((1, 16, 128), BF)]
    )

    owner_flat = owner[:, 0]
    slab = owner_flat.shape[0]
    numbers = jnp.arange(slab, dtype=jnp.int32)
    earlier = (owner_flat[None, :] == owner_flat[:, None]) & (numbers[None, :] < numbers[:, None])
    position = jnp.sum(earlier.astype(jnp.int32), axis=1)
    slots = owner_flat * CAP + position
    distance = (numbers // 16 - z + 4) % 4
    at = jnp.where((numbers // 8) % 2 == c, 0, 32) + distance * 8 + numbers % 8
    match = slots[None, :] == jnp.arange(32 * CAP, dtype=jnp.int32)[:, None]
    source = jnp.min(jnp.where(match, at[None, :], 64), axis=1)
    outgoing = fill_slots(source, pieces)
    arrived = lax.all_to_all(
        outgoing.reshape(32, CAP, 16, 128), "sub", split_axis=0, concat_axis=0, tiled=True
    )
    arrived = arrived.reshape(16, 2, CAP, 16, 128).transpose(2, 0, 3, 1, 4)
    return arrived.reshape(1, CAP, 256, 256).astype(F32)


def solution(mesh):
    in_specs = (
        P("grp", "sub", None),
        P("sub", None),
        P("sub", "grp"),
        P("sub", "grp"),
        P("grp", "sub"),
        P("grp", "sub"),
        P(),
    )
    out_specs = P("grp", "sub", None, None)
    return jax.shard_map(
        per_device, mesh=mesh, in_specs=in_specs, out_specs=out_specs, check_vma=False
    )
```

```python
import jax
import jax.numpy as jnp
from jax import lax
from jax.experimental import pallas as pl
from jax.experimental.pallas import tpu as pltpu
from jax.sharding import PartitionSpec as P

CAP = 3
AXES = ("grp", "sub")
BF = jnp.bfloat16
F32 = jnp.float32
MIB = 1024 * 1024
STACK = 4


def pairs(target):
    out = []
    for z in range(4):
        for x in range(4):
            for y in range(4):
                for c in range(2):
                    tz, tx, ty, tc = target(z, x, y, c)
                    to = (tz % 4) * 32 + ((tx % 4) * 4 + ty % 4) * 2 + tc
                    out.append((z * 32 + (x * 4 + y) * 2 + c, to))
    return out


def along(number, d):
    def target(z, x, y, c):
        return (z, x + d, y, c) if c == number else (z, x, y + d, c)

    return pairs(target)


CORE = pairs(lambda z, x, y, c: (z, x, y, 1 - c))
FIRST = [along(0, d) for d in range(4)]
SECOND = [along(1, d) for d in range(4)]
DEPTH = [pairs(lambda z, x, y, c, d=d: (z + d, x, y, c)) for d in range(4)]


def move(value, permutation):
    return lax.ppermute(value, AXES, permutation)


def tie(*values):
    return lax.optimization_barrier(values)


def whole(shape):
    return pl.BlockSpec(shape, lambda *_: (0,) * len(shape))


def pick_body(sc, set0, set1, set2, set3, out, sem):
    c = sc[0]
    for k in range(4):
        block = sc[3 + k]
        tx, ty, tc = block // 8, (block // 2) % 4, block % 2
        t1 = jnp.where(c == 0, tx, ty)
        t2 = jnp.where(c == 0, ty, tx)
        at = ((sc[1] - t1 + 4) % 4) * 2 + tc
        far = (sc[2] - t2 + 4) % 4
        for e, source in enumerate((set0, set1, set2, set3)):

            @pl.when(far == e)
            def _(source=source):
                pltpu.make_async_copy(source.at[at], out.at[k], sem.at[k]).start()

    for k in range(4):
        pltpu.make_async_copy(set0.at[0], out.at[k], sem.at[k]).wait()


def pick(scalars, *sets):
    return pl.pallas_call(
        pick_body,
        grid_spec=pltpu.PrefetchScalarGridSpec(
            num_scalar_prefetch=1,
            grid=(1,),
            in_specs=[pl.BlockSpec(memory_space=pl.ANY)] * 4,
            out_specs=whole((4, 128, 256)),
            scratch_shapes=[pltpu.SemaphoreType.DMA((4,))],
        ),
        out_shape=jax.ShapeDtypeStruct((4, 128, 256), BF),
        compiler_params=pltpu.CompilerParams(vmem_limit_bytes=4 * MIB),
        cost_estimate=pl.CostEstimate(flops=0, bytes_accessed=1000, transcendentals=0),
    )(scalars, *sets)


def order_body(sc, own, oth, out):
    for k in range(16):
        rows = pl.ds(pl.multiple_of(sc[k] * 16, 16), 16)
        to = slice(k * 16, (k + 1) * 16)
        for r in range(out.shape[0]):
            out[r, to, 0:256] = own[r, rows, :]
            out[r, to, 256:512] = oth[r, rows, :]


def order_rows(strips, own, oth):
    count = own.shape[0]
    return pl.pallas_call(
        order_body,
        grid_spec=pltpu.PrefetchScalarGridSpec(
            num_scalar_prefetch=1,
            grid=(1,),
            in_specs=[whole((count, 256, 256))] * 2,
            out_specs=whole((count, 256, 512)),
        ),
        out_shape=jax.ShapeDtypeStruct((count, 256, 512), BF),
        compiler_params=pltpu.CompilerParams(vmem_limit_bytes=8 * MIB),
        cost_estimate=pl.CostEstimate(flops=0, bytes_accessed=1000, transcendentals=0),
    )(strips, own, oth)


def products_body(sc, t_own, t_oth, gv, *refs):
    halves, (send1, send2, send3, keep, go) = refs[: 2 * gv.shape[0]], refs[-5:]
    count = len(halves) // 2
    c = sc[0]

    @pl.when(pl.program_id(0) == 0)
    def _():
        for r in range(count):
            for n, half in enumerate((c, 1 - c)):
                for k in range(4):
                    rows = pl.ds(pl.multiple_of((k % 2) * 256 + half * 128, 128), 128)
                    go[2 * r + k // 2, rows, :] = halves[2 * r + n][k]

    for r in range(count):
        half_own = jnp.dot(
            t_own[...].reshape(STACK * 256, 512), go[2 * r + c], preferred_element_type=F32
        ).astype(BF)
        half_oth = jnp.dot(
            t_oth[...].reshape(STACK * 256, 512), go[2 * r + 1 - c], preferred_element_type=F32
        ).astype(BF)
        for p in range(STACK):
            rows = slice(p * 256, (p + 1) * 256)
            out = jnp.dot(gv[r, :, 0:256], half_own[rows], preferred_element_type=F32)
            out += jnp.dot(gv[r, :, 256:512], half_oth[rows], preferred_element_type=F32)
            send1[p, r] = out[0:64].astype(BF)
            send2[p, r] = out[64:128].astype(BF)
            send3[p, r] = out[128:192].astype(BF)
            keep[p, r] = out[192:256]


def products_of(core, t_own, t_oth, gv, halves, room, at, gv_at, begun=()):
    count = len(halves) // 2
    block = pl.BlockSpec((STACK, count, 64, 256), lambda p, sc: (p, at, 0, 0))
    shape = (8, room, 64, 256)
    first = 4 + 2 * count
    functions = pl.BlockSpec((STACK, 256, 512), lambda p, sc: (sc[0] * (8 // STACK) + p, 0, 0))
    return pl.pallas_call(
        products_body,
        grid_spec=pltpu.PrefetchScalarGridSpec(
            num_scalar_prefetch=1,
            grid=(8 // STACK,),
            in_specs=[functions] * 2
            + [pl.BlockSpec((count, 256, 512), lambda p, sc: (gv_at, 0, 0))]
            + [whole((4, 128, 256))] * (2 * count)
            + [pl.BlockSpec(memory_space=pl.ANY)] * len(begun),
            out_specs=[block] * 4,
            scratch_shapes=[pltpu.VMEM((2 * count, 512, 256), BF)],
        ),
        out_shape=[jax.ShapeDtypeStruct(shape, BF)] * 3 + [jax.ShapeDtypeStruct(shape, F32)],
        input_output_aliases={first + n: n for n in range(len(begun))},
        compiler_params=pltpu.CompilerParams(vmem_limit_bytes=(12 + 4 * count) * MIB),
        cost_estimate=pl.CostEstimate(flops=1000, bytes_accessed=1000, transcendentals=0),
    )(core, pltpu.with_memory_space_constraint(t_own, pltpu.HBM), t_oth, gv, *halves, *begun)


def slots_body(sc, pieces, out):
    for s in range(32 * CAP):
        out[s] = pieces[sc[s]]


def fill_slots(source, pieces):
    return pl.pallas_call(
        slots_body,
        grid_spec=pltpu.PrefetchScalarGridSpec(
            num_scalar_prefetch=1,
            grid=(1,),
            in_specs=[whole((65, 16, 128))],
            out_specs=whole((32 * CAP, 16, 128)),
        ),
        out_shape=jax.ShapeDtypeStruct((32 * CAP, 16, 128), BF),
        compiler_params=pltpu.CompilerParams(vmem_limit_bytes=4 * MIB),
    )(source, pieces)


def widen_body(pieces, out):
    for n in range(32):
        rows, columns = slice(n // 2 * 16, n // 2 * 16 + 16), slice(n % 2 * 128, n % 2 * 128 + 128)
        for k in range(CAP):
            out[k, rows, columns] = pieces[n, k].astype(F32)


def widen(pieces):
    return pl.pallas_call(
        widen_body,
        in_specs=[pl.BlockSpec(memory_space=pltpu.VMEM)],
        out_specs=pl.BlockSpec(memory_space=pltpu.VMEM),
        out_shape=jax.ShapeDtypeStruct((CAP, 256, 256), F32),
        compiler_params=pltpu.CompilerParams(vmem_limit_bytes=8 * MIB),
    )(pieces)


def per_device(three_centre, pair_blocks, green_occ, occ_mask, green_virt, virt_mask, owner):
    z = lax.axis_index("grp")
    sub = lax.axis_index("sub")
    x, y, c = sub // 8, (sub // 2) % 4, sub % 2
    q1, q2 = jnp.where(c == 0, x, y), jnp.where(c == 0, y, x)

    def by_core(mine, other):
        return jnp.where(c == 0, jnp.stack([mine, other]), jnp.stack([other, mine]))

    go = green_occ * occ_mask[0, 0].astype(BF)
    go = by_core(
        lax.dynamic_slice_in_dim(go, c * 128, 128, 0),
        move(lax.dynamic_slice_in_dim(go, (1 - c) * 128, 128, 0), CORE),
    )
    go, theirs = tie(go, three_centre)
    t_oth = move(theirs, CORE)

    go1, go3, go2 = [move(go, FIRST[d]) for d in (1, 3, 2)]
    near = jnp.concatenate([go, go1, go2, go3])
    near, gv = tie(near, green_virt * virt_mask[0, 0].astype(BF))
    gv1, gv3, gv2 = [move(gv, DEPTH[r]) for r in (1, 3, 2)]
    set1, set3, set2 = [move(near, SECOND[e]) for e in (1, 3, 2)]
    gv = gv.reshape(1, 256, 256)
    strips = jnp.stack(
        [
            jnp.where(c == 0, s1 * 4 + s2, s2 * 4 + s1)
            for s1 in [(q1 + d) % 4 for d in (1, 2, 3, 0)]
            for s2 in [(q2 + e) % 4 for e in range(4)]
        ]
    ).astype(jnp.int32)
    gv = order_rows(strips, gv, move(gv, CORE))

    partners = by_core(pair_blocks[0], move(pair_blocks, CORE)[0]).reshape(4)
    places = jnp.concatenate([jnp.stack([c, q1, q2]), partners]).astype(jnp.int32)
    places, gv, set1, set3, set2 = tie(places, gv, set1, set3, set2)
    picked = pick(places, near, set1, set2, set3)
    gv1, gv3, gv2, picked = tie(gv1, gv3, gv2, picked)
    gv_rest = jnp.stack([gv1, gv3, gv2])
    gv_rest = order_rows(strips, gv_rest, move(gv_rest, CORE))
    far, *side = [move(picked, DEPTH[r]) for r in (2, 3, 1)]

    given = (c.reshape(1).astype(jnp.int32), three_centre, t_oth)
    sends0 = products_of(*given, gv, (picked, move(picked, CORE)), 1, 0, 0)
    *sends0, side3, side1 = tie(*sends0, *side)
    got0 = [move(sends0[d - 1], FIRST[d]) for d in (1, 3, 2)]
    halves = [h for a in (side1, side3) for h in (a, move(a, CORE))]
    sends1 = products_of(*given, gv_rest, halves, 2, 0, 0)
    *sends1, far = tie(*sends1, far)
    *got0, far = tie(*got0, far)
    sends2 = products_of(*given, gv_rest, (far, move(far, CORE)), 1, 0, 2)

    def sum_of(sends, got):
        total = sends[3]
        for part in got:
            total = total + part.astype(F32)
        return total

    got1 = [move(sends1[d - 1], FIRST[d]) for d in (1, 3, 2)]
    got2 = [move(sends2[d - 1], FIRST[d]) for d in (1, 3, 2)]
    sums = [sum_of(sends0, got0), sum_of(sends1, got1), sum_of(sends2, got2)]

    def strip(e):
        return jnp.concatenate([t[:, :, e * 16 : (e + 1) * 16] for t in sums], axis=1)

    total = strip(0)
    for e in (1, 3, 2):
        total = total + move(strip(e).astype(BF), SECOND[e]).astype(F32)
    total = total.astype(BF)

    rows = jnp.stack(
        [total[:, 0]] + [move(total[:, at], DEPTH[4 - r]) for at, r in ((1, 1), (2, 3), (3, 2))]
    )
    mine = lax.dynamic_slice_in_dim(rows, c * 128, 128, 3)
    other = move(lax.dynamic_slice_in_dim(rows, (1 - c) * 128, 128, 3), CORE)
    pieces = jnp.concatenate(
        [mine.reshape(32, 16, 128), other.reshape(32, 16, 128), jnp.zeros((1, 16, 128), BF)]
    )

    owner_flat = owner[:, 0]
    slab = owner_flat.shape[0]
    numbers = jnp.arange(slab, dtype=jnp.int32)
    earlier = (owner_flat[None, :] == owner_flat[:, None]) & (numbers[None, :] < numbers[:, None])
    position = jnp.sum(earlier.astype(jnp.int32), axis=1)
    slots = owner_flat * CAP + position
    distance = (numbers // 16 - z + 4) % 4
    stands = distance ^ (distance >> 1)
    at = jnp.where((numbers // 8) % 2 == c, 0, 32) + stands * 8 + numbers % 8
    match = slots[None, :] == jnp.arange(32 * CAP, dtype=jnp.int32)[:, None]
    source = jnp.min(jnp.where(match, at[None, :], 64), axis=1)
    outgoing = fill_slots(source, pieces)
    arrived = lax.all_to_all(
        outgoing.reshape(32, CAP, 16, 128), "sub", split_axis=0, concat_axis=0, tiled=True
    )
    return widen(arrived).reshape(1, CAP, 256, 256)


def solution(mesh):
    in_specs = (
        P("grp", "sub", None),
        P("sub", None),
        P("sub", "grp"),
        P("sub", "grp"),
        P("grp", "sub"),
        P("grp", "sub"),
        P(),
    )
    out_specs = P("grp", "sub", None, None)
    return jax.shard_map(
        per_device, mesh=mesh, in_specs=in_specs, out_specs=out_specs, check_vma=False
    )
```

```python
import jax
import jax.numpy as jnp
from jax import lax
from jax.experimental import pallas as pl
from jax.experimental.pallas import tpu as pltpu
from jax.sharding import PartitionSpec as P

CAP = 3
AXES = ("grp", "sub")
BF = jnp.bfloat16
F32 = jnp.float32
MIB = 1024 * 1024
STACK = 4


def pairs(target):
    out = []
    for z in range(4):
        for x in range(4):
            for y in range(4):
                for c in range(2):
                    tz, tx, ty, tc = target(z, x, y, c)
                    to = (tz % 4) * 32 + ((tx % 4) * 4 + ty % 4) * 2 + tc
                    out.append((z * 32 + (x * 4 + y) * 2 + c, to))
    return out


def along(number, d):
    def target(z, x, y, c):
        return (z, x + d, y, c) if c == number else (z, x, y + d, c)

    return pairs(target)


CORE = pairs(lambda z, x, y, c: (z, x, y, 1 - c))
FIRST = [along(0, d) for d in range(4)]
SECOND = [along(1, d) for d in range(4)]
DEPTH = [pairs(lambda z, x, y, c, d=d: (z + d, x, y, c)) for d in range(4)]


def move(value, permutation):
    return lax.ppermute(value, AXES, permutation)


def tie(*values):
    return lax.optimization_barrier(values)


def whole(shape):
    return pl.BlockSpec(shape, lambda *_: (0,) * len(shape))


def pick_body(sc, set0, set1, set2, set3, out, sem):
    c = sc[0]
    for k in range(4):
        block = sc[3 + k]
        tx, ty, tc = block // 8, (block // 2) % 4, block % 2
        t1 = jnp.where(c == 0, tx, ty)
        t2 = jnp.where(c == 0, ty, tx)
        at = ((sc[1] - t1 + 4) % 4) * 2 + tc
        far = (sc[2] - t2 + 4) % 4
        for e, source in enumerate((set0, set1, set2, set3)):

            @pl.when(far == e)
            def _(source=source):
                pltpu.make_async_copy(source.at[at], out.at[k], sem.at[k]).start()

    for k in range(4):
        pltpu.make_async_copy(set0.at[0], out.at[k], sem.at[k]).wait()


def pick(scalars, *sets):
    return pl.pallas_call(
        pick_body,
        grid_spec=pltpu.PrefetchScalarGridSpec(
            num_scalar_prefetch=1,
            grid=(1,),
            in_specs=[pl.BlockSpec(memory_space=pl.ANY)] * 4,
            out_specs=whole((4, 128, 256)),
            scratch_shapes=[pltpu.SemaphoreType.DMA((4,))],
        ),
        out_shape=jax.ShapeDtypeStruct((4, 128, 256), BF),
        compiler_params=pltpu.CompilerParams(vmem_limit_bytes=4 * MIB),
        cost_estimate=pl.CostEstimate(flops=0, bytes_accessed=1000, transcendentals=0),
    )(scalars, *sets)


def order_body(sc, own, oth, out):
    for k in range(16):
        rows = pl.ds(pl.multiple_of(sc[k] * 16, 16), 16)
        to = slice(k * 16, (k + 1) * 16)
        for r in range(out.shape[0]):
            out[r, to, 0:256] = own[r, rows, :]
            out[r, to, 256:512] = oth[r, rows, :]


def order_rows(strips, own, oth):
    count = own.shape[0]
    return pl.pallas_call(
        order_body,
        grid_spec=pltpu.PrefetchScalarGridSpec(
            num_scalar_prefetch=1,
            grid=(1,),
            in_specs=[whole((count, 256, 256))] * 2,
            out_specs=whole((count, 256, 512)),
        ),
        out_shape=jax.ShapeDtypeStruct((count, 256, 512), BF),
        compiler_params=pltpu.CompilerParams(vmem_limit_bytes=8 * MIB),
        cost_estimate=pl.CostEstimate(flops=0, bytes_accessed=1000, transcendentals=0),
    )(strips, own, oth)


def keep_half_body(sc, own, oth, out_own, out_oth, sem):
    rows = pl.ds(sc[0] * 8, 8)
    copies = [
        pltpu.make_async_copy(own.at[rows], out_own, sem.at[0]),
        pltpu.make_async_copy(oth.at[rows], out_oth, sem.at[1]),
    ]
    for copy in copies:
        copy.start()
    for copy in copies:
        copy.wait()


def keep_half(core, own, oth):
    shape = jax.ShapeDtypeStruct((8, 256, 512), BF)
    return pl.pallas_call(
        keep_half_body,
        in_specs=[pl.BlockSpec(memory_space=pltpu.SMEM)] + [pl.BlockSpec(memory_space=pl.ANY)] * 2,
        out_specs=[pl.BlockSpec(memory_space=pltpu.VMEM)] * 2,
        scratch_shapes=[pltpu.SemaphoreType.DMA((2,))],
        out_shape=[shape, shape],
        compiler_params=pltpu.CompilerParams(vmem_limit_bytes=10 * MIB),
        cost_estimate=pl.CostEstimate(flops=0, bytes_accessed=1000, transcendentals=0),
    )(core, *[pltpu.with_memory_space_constraint(t, pltpu.HBM) for t in (own, oth)])


def products_body(sc, t_own, t_oth, gv, *refs):
    halves, (send1, send2, send3, keep, go) = refs[: 2 * gv.shape[0]], refs[-5:]
    count = len(halves) // 2
    c = sc[0]

    @pl.when(pl.program_id(0) == 0)
    def _():
        for r in range(count):
            for n, half in enumerate((c, 1 - c)):
                for k in range(4):
                    rows = pl.ds(pl.multiple_of((k % 2) * 256 + half * 128, 128), 128)
                    go[2 * r + k // 2, rows, :] = halves[2 * r + n][k]

    for r in range(count):
        half_own = jnp.dot(
            t_own[...].reshape(STACK * 256, 512), go[2 * r + c], preferred_element_type=F32
        ).astype(BF)
        half_oth = jnp.dot(
            t_oth[...].reshape(STACK * 256, 512), go[2 * r + 1 - c], preferred_element_type=F32
        ).astype(BF)
        for p in range(STACK):
            rows = slice(p * 256, (p + 1) * 256)
            out = jnp.dot(gv[r, :, 0:256], half_own[rows], preferred_element_type=F32)
            out += jnp.dot(gv[r, :, 256:512], half_oth[rows], preferred_element_type=F32)
            send1[r, p] = out[0:64].astype(BF)
            send2[r, p] = out[64:128].astype(BF)
            send3[r, p] = out[128:192].astype(BF)
            keep[r, p] = out[192:256]


def products_of(core, t_own, t_oth, gv, halves, room, at, gv_at, begun=()):
    count = len(halves) // 2
    block = pl.BlockSpec((count, STACK, 64, 256), lambda p, sc: (at, p, 0, 0))
    shape = (room, 8, 64, 256)
    first = 4 + 2 * count
    functions = pl.BlockSpec((STACK, 256, 512), lambda p, sc: (p, 0, 0))
    return pl.pallas_call(
        products_body,
        grid_spec=pltpu.PrefetchScalarGridSpec(
            num_scalar_prefetch=1,
            grid=(8 // STACK,),
            in_specs=[functions] * 2
            + [pl.BlockSpec((count, 256, 512), lambda p, sc: (gv_at, 0, 0))]
            + [whole((4, 128, 256))] * (2 * count)
            + [pl.BlockSpec(memory_space=pl.ANY)] * len(begun),
            out_specs=[block] * 4,
            scratch_shapes=[pltpu.VMEM((2 * count, 512, 256), BF)],
        ),
        out_shape=[jax.ShapeDtypeStruct(shape, BF)] * 3 + [jax.ShapeDtypeStruct(shape, F32)],
        input_output_aliases={first + n: n for n in range(len(begun))},
        compiler_params=pltpu.CompilerParams(vmem_limit_bytes=(12 + 4 * count) * MIB),
        cost_estimate=pl.CostEstimate(flops=1000, bytes_accessed=1000, transcendentals=0),
    )(core, t_own, t_oth, gv, *halves, *begun)


def slots_body(sc, pieces, out):
    for s in range(32 * CAP):
        out[s] = pieces[sc[s]]


def fill_slots(source, pieces):
    return pl.pallas_call(
        slots_body,
        grid_spec=pltpu.PrefetchScalarGridSpec(
            num_scalar_prefetch=1,
            grid=(1,),
            in_specs=[whole((65, 16, 128))],
            out_specs=whole((32 * CAP, 16, 128)),
        ),
        out_shape=jax.ShapeDtypeStruct((32 * CAP, 16, 128), BF),
        compiler_params=pltpu.CompilerParams(vmem_limit_bytes=4 * MIB),
    )(source, pieces)


def widen_body(pieces, out):
    for n in range(32):
        rows, columns = slice(n // 2 * 16, n // 2 * 16 + 16), slice(n % 2 * 128, n % 2 * 128 + 128)
        for k in range(CAP):
            out[k, rows, columns] = pieces[n, k].astype(F32)


def widen(pieces):
    return pl.pallas_call(
        widen_body,
        in_specs=[pl.BlockSpec(memory_space=pltpu.VMEM)],
        out_specs=pl.BlockSpec(memory_space=pltpu.VMEM),
        out_shape=jax.ShapeDtypeStruct((CAP, 256, 256), F32),
        compiler_params=pltpu.CompilerParams(vmem_limit_bytes=8 * MIB),
    )(pieces)


def per_device(three_centre, pair_blocks, green_occ, occ_mask, green_virt, virt_mask, owner):
    z = lax.axis_index("grp")
    sub = lax.axis_index("sub")
    x, y, c = sub // 8, (sub // 2) % 4, sub % 2
    q1, q2 = jnp.where(c == 0, x, y), jnp.where(c == 0, y, x)

    def by_core(mine, other):
        return jnp.where(c == 0, jnp.stack([mine, other]), jnp.stack([other, mine]))

    go = green_occ * occ_mask[0, 0].astype(BF)
    go = by_core(
        lax.dynamic_slice_in_dim(go, c * 128, 128, 0),
        move(lax.dynamic_slice_in_dim(go, (1 - c) * 128, 128, 0), CORE),
    )
    go, theirs = tie(go, three_centre)
    t_oth = move(theirs, CORE)

    go1, go3, go2 = [move(go, FIRST[d]) for d in (1, 3, 2)]
    near = jnp.concatenate([go, go1, go2, go3])
    near, gv = tie(near, green_virt * virt_mask[0, 0].astype(BF))
    gv1, gv3, gv2 = [move(gv, DEPTH[r]) for r in (1, 3, 2)]
    set1, set3, set2 = [move(near, SECOND[e]) for e in (1, 3, 2)]
    gv = gv.reshape(1, 256, 256)
    strips = jnp.stack(
        [
            jnp.where(c == 0, s1 * 4 + s2, s2 * 4 + s1)
            for s1 in [(q1 + d) % 4 for d in (1, 2, 3, 0)]
            for s2 in [(q2 + e) % 4 for e in range(4)]
        ]
    ).astype(jnp.int32)
    gv = order_rows(strips, gv, move(gv, CORE))

    partners = by_core(pair_blocks[0], move(pair_blocks, CORE)[0]).reshape(4)
    places = jnp.concatenate([jnp.stack([c, q1, q2]), partners]).astype(jnp.int32)
    places, gv, set1, set3, set2 = tie(places, gv, set1, set3, set2)
    picked = pick(places, near, set1, set2, set3)
    gv1, gv3, gv2, picked = tie(gv1, gv3, gv2, picked)
    gv_rest = jnp.stack([gv1, gv3, gv2])
    gv_rest = order_rows(strips, gv_rest, move(gv_rest, CORE))
    far, *side = [move(picked, DEPTH[r]) for r in (2, 3, 1)]

    core = c.reshape(1).astype(jnp.int32)
    given = (core, *keep_half(core, three_centre, t_oth))
    sends0 = products_of(*given, gv, (picked, move(picked, CORE)), 1, 0, 0)
    *sends0, side3, side1 = tie(*sends0, *side)
    got0 = [move(sends0[d - 1], FIRST[d]) for d in (2, 1, 3)]
    halves = [h for a in (side1, side3) for h in (a, move(a, CORE))]
    sends1 = products_of(*given, gv_rest, halves, 2, 0, 0)
    *sends1, far = tie(*sends1, far)
    *got0, far = tie(*got0, far)
    sends2 = products_of(*given, gv_rest, (far, move(far, CORE)), 1, 0, 2)

    def sum_of(sends, got):
        total = sends[3]
        for part in got:
            total = total + part.astype(F32)
        return total

    got1 = [move(sends1[d - 1], FIRST[d]) for d in (2, 1, 3)]
    got2 = [move(sends2[d - 1], FIRST[d]) for d in (2, 1, 3)]
    sums = [sum_of(sends0, got0), sum_of(sends1, got1), sum_of(sends2, got2)]

    def strip(e):
        return jnp.concatenate([t[:, :, e * 16 : (e + 1) * 16] for t in sums])

    total = strip(0)
    for e in (2, 1, 3):
        total = total + move(strip(e).astype(BF), SECOND[e]).astype(F32)
    total = total.astype(BF)

    rows = jnp.stack(
        [total[0]] + [move(total[at], DEPTH[4 - r]) for at, r in ((3, 2), (1, 1), (2, 3))]
    )
    mine = lax.dynamic_slice_in_dim(rows, c * 128, 128, 3)
    other = move(lax.dynamic_slice_in_dim(rows, (1 - c) * 128, 128, 3), CORE)
    pieces = jnp.concatenate(
        [mine.reshape(32, 16, 128), other.reshape(32, 16, 128), jnp.zeros((1, 16, 128), BF)]
    )

    owner_flat = owner[:, 0]
    slab = owner_flat.shape[0]
    numbers = jnp.arange(slab, dtype=jnp.int32)
    earlier = (owner_flat[None, :] == owner_flat[:, None]) & (numbers[None, :] < numbers[:, None])
    position = jnp.sum(earlier.astype(jnp.int32), axis=1)
    slots = owner_flat * CAP + position
    distance = (numbers // 16 - z + 4) % 4
    stands = (distance % 2) * 2 + distance // 2
    at = jnp.where((numbers // 8) % 2 == c, 0, 32) + stands * 8 + numbers % 8
    match = slots[None, :] == jnp.arange(32 * CAP, dtype=jnp.int32)[:, None]
    source = jnp.min(jnp.where(match, at[None, :], 64), axis=1)
    outgoing = fill_slots(source, pieces)
    arrived = lax.all_to_all(
        outgoing.reshape(32, CAP, 16, 128), "sub", split_axis=0, concat_axis=0, tiled=True
    )
    return widen(arrived).reshape(1, CAP, 256, 256)


def solution(mesh):
    in_specs = (
        P("grp", "sub", None),
        P("sub", None),
        P("sub", "grp"),
        P("sub", "grp"),
        P("grp", "sub"),
        P("grp", "sub"),
        P(),
    )
    out_specs = P("grp", "sub", None, None)
    return jax.shard_map(
        per_device, mesh=mesh, in_specs=in_specs, out_specs=out_specs, check_vma=False
    )
```

```python
import jax
import jax.numpy as jnp
from jax import lax
from jax.experimental import pallas as pl
from jax.experimental.pallas import tpu as pltpu
from jax.sharding import PartitionSpec as P

CAP = 3
AXES = ("grp", "sub")
BF = jnp.bfloat16
F32 = jnp.float32
MIB = 1024 * 1024
STACK = 4


def pairs(target):
    out = []
    for z in range(4):
        for x in range(4):
            for y in range(4):
                for c in range(2):
                    tz, tx, ty, tc = target(z, x, y, c)
                    to = (tz % 4) * 32 + ((tx % 4) * 4 + ty % 4) * 2 + tc
                    out.append((z * 32 + (x * 4 + y) * 2 + c, to))
    return out


def along(number, d):
    def target(z, x, y, c):
        return (z, x + d, y, c) if c == number else (z, x, y + d, c)

    return pairs(target)


CORE = pairs(lambda z, x, y, c: (z, x, y, 1 - c))
FIRST = [along(0, d) for d in range(4)]
SECOND = [along(1, d) for d in range(4)]
DEPTH = [pairs(lambda z, x, y, c, d=d: (z + d, x, y, c)) for d in range(4)]


def move(value, permutation):
    return lax.ppermute(value, AXES, permutation)


def tie(*values):
    return lax.optimization_barrier(values)


def whole(shape):
    return pl.BlockSpec(shape, lambda *_: (0,) * len(shape))


def pick_body(sc, set0, set1, set2, set3, out, sem):
    c = sc[0]
    for k in range(4):
        block = sc[3 + k]
        tx, ty, tc = block // 8, (block // 2) % 4, block % 2
        t1 = jnp.where(c == 0, tx, ty)
        t2 = jnp.where(c == 0, ty, tx)
        at = ((sc[1] - t1 + 4) % 4) * 2 + tc
        far = (sc[2] - t2 + 4) % 4
        for e, source in enumerate((set0, set1, set2, set3)):

            @pl.when(far == e)
            def _(source=source):
                pltpu.make_async_copy(source.at[at], out.at[k], sem.at[k]).start()

    for k in range(4):
        pltpu.make_async_copy(set0.at[0], out.at[k], sem.at[k]).wait()


def pick(scalars, *sets):
    return pl.pallas_call(
        pick_body,
        grid_spec=pltpu.PrefetchScalarGridSpec(
            num_scalar_prefetch=1,
            grid=(1,),
            in_specs=[pl.BlockSpec(memory_space=pl.ANY)] * 4,
            out_specs=whole((4, 128, 256)),
            scratch_shapes=[pltpu.SemaphoreType.DMA((4,))],
        ),
        out_shape=jax.ShapeDtypeStruct((4, 128, 256), BF),
        compiler_params=pltpu.CompilerParams(vmem_limit_bytes=4 * MIB),
        cost_estimate=pl.CostEstimate(flops=0, bytes_accessed=1000, transcendentals=0),
    )(scalars, *sets)


def order_body(sc, own, oth, out):
    for k in range(16):
        rows = pl.ds(pl.multiple_of(sc[k] * 16, 16), 16)
        to = slice(k * 16, (k + 1) * 16)
        for r in range(out.shape[0]):
            out[r, to, 0:256] = own[r, rows, :]
            out[r, to, 256:512] = oth[r, rows, :]


def order_rows(strips, own, oth):
    count = own.shape[0]
    return pl.pallas_call(
        order_body,
        grid_spec=pltpu.PrefetchScalarGridSpec(
            num_scalar_prefetch=1,
            grid=(1,),
            in_specs=[whole((count, 256, 256))] * 2,
            out_specs=whole((count, 256, 512)),
        ),
        out_shape=jax.ShapeDtypeStruct((count, 256, 512), BF),
        compiler_params=pltpu.CompilerParams(vmem_limit_bytes=8 * MIB),
        cost_estimate=pl.CostEstimate(flops=0, bytes_accessed=1000, transcendentals=0),
    )(strips, own, oth)


def keep_half_body(sc, own, oth, out_own, out_oth, sem):
    rows = pl.ds(sc[0] * 8, 8)
    copies = [
        pltpu.make_async_copy(own.at[rows], out_own, sem.at[0]),
        pltpu.make_async_copy(oth.at[rows], out_oth, sem.at[1]),
    ]
    for copy in copies:
        copy.start()
    for copy in copies:
        copy.wait()


def keep_half(core, own, oth):
    shape = jax.ShapeDtypeStruct((8, 256, 512), BF)
    return pl.pallas_call(
        keep_half_body,
        in_specs=[pl.BlockSpec(memory_space=pltpu.SMEM)] + [pl.BlockSpec(memory_space=pl.ANY)] * 2,
        out_specs=[pl.BlockSpec(memory_space=pltpu.VMEM)] * 2,
        scratch_shapes=[pltpu.SemaphoreType.DMA((2,))],
        out_shape=[shape, shape],
        compiler_params=pltpu.CompilerParams(vmem_limit_bytes=10 * MIB),
        cost_estimate=pl.CostEstimate(flops=0, bytes_accessed=1000, transcendentals=0),
    )(core, *[pltpu.with_memory_space_constraint(t, pltpu.HBM) for t in (own, oth)])


def products_body(sc, t_own, t_oth, gv, *refs):
    halves, (send1, send2, send3, keep, go) = refs[: 2 * gv.shape[0]], refs[-5:]
    count = len(halves) // 2
    c = sc[0]

    @pl.when(pl.program_id(0) == 0)
    def _():
        for r in range(count):
            for n, half in enumerate((c, 1 - c)):
                for k in range(4):
                    rows = pl.ds(pl.multiple_of((k % 2) * 256 + half * 128, 128), 128)
                    go[2 * r + k // 2, rows, :] = halves[2 * r + n][k]

    for r in range(count):
        half_own = jnp.dot(
            t_own[...].reshape(STACK * 256, 512), go[2 * r + c], preferred_element_type=F32
        ).astype(BF)
        half_oth = jnp.dot(
            t_oth[...].reshape(STACK * 256, 512), go[2 * r + 1 - c], preferred_element_type=F32
        ).astype(BF)
        for p in range(STACK):
            rows = slice(p * 256, (p + 1) * 256)
            out = jnp.dot(gv[r, :, 0:256], half_own[rows], preferred_element_type=F32)
            out += jnp.dot(gv[r, :, 256:512], half_oth[rows], preferred_element_type=F32)
            send1[r, p] = out[0:64].astype(BF)
            send2[r, p] = out[64:128].astype(BF)
            send3[r, p] = out[128:192].astype(BF)
            keep[r, p] = out[192:256]


def products_of(core, t_own, t_oth, gv, halves, room, at, gv_at, begun=()):
    count = len(halves) // 2
    block = pl.BlockSpec((count, STACK, 64, 256), lambda p, sc: (at, p, 0, 0))
    shape = (room, 8, 64, 256)
    first = 4 + 2 * count
    functions = pl.BlockSpec((STACK, 256, 512), lambda p, sc: (p, 0, 0))
    return pl.pallas_call(
        products_body,
        grid_spec=pltpu.PrefetchScalarGridSpec(
            num_scalar_prefetch=1,
            grid=(8 // STACK,),
            in_specs=[functions] * 2
            + [pl.BlockSpec((count, 256, 512), lambda p, sc: (gv_at, 0, 0))]
            + [whole((4, 128, 256))] * (2 * count)
            + [pl.BlockSpec(memory_space=pl.ANY)] * len(begun),
            out_specs=[block] * 4,
            scratch_shapes=[pltpu.VMEM((2 * count, 512, 256), BF)],
        ),
        out_shape=[jax.ShapeDtypeStruct(shape, BF)] * 3 + [jax.ShapeDtypeStruct(shape, F32)],
        input_output_aliases={first + n: n for n in range(len(begun))},
        compiler_params=pltpu.CompilerParams(vmem_limit_bytes=(12 + 4 * count) * MIB),
        cost_estimate=pl.CostEstimate(flops=1000, bytes_accessed=1000, transcendentals=0),
    )(core, t_own, t_oth, gv, *halves, *begun)


def slots_body(sc, pieces, out):
    for s in range(32 * CAP):
        out[s] = pieces[sc[s]]


def fill_slots(source, pieces):
    return pl.pallas_call(
        slots_body,
        grid_spec=pltpu.PrefetchScalarGridSpec(
            num_scalar_prefetch=1,
            grid=(1,),
            in_specs=[whole((65, 16, 128))],
            out_specs=whole((32 * CAP, 16, 128)),
        ),
        out_shape=jax.ShapeDtypeStruct((32 * CAP, 16, 128), BF),
        compiler_params=pltpu.CompilerParams(vmem_limit_bytes=4 * MIB),
    )(source, pieces)


def widen_body(pieces, out):
    for n in range(32):
        rows, columns = slice(n // 2 * 16, n // 2 * 16 + 16), slice(n % 2 * 128, n % 2 * 128 + 128)
        for k in range(CAP):
            out[k, rows, columns] = pieces[n, k].astype(F32)


def widen(pieces):
    return pl.pallas_call(
        widen_body,
        in_specs=[pl.BlockSpec(memory_space=pltpu.VMEM)],
        out_specs=pl.BlockSpec(memory_space=pltpu.VMEM),
        out_shape=jax.ShapeDtypeStruct((CAP, 256, 256), F32),
        compiler_params=pltpu.CompilerParams(vmem_limit_bytes=8 * MIB),
    )(pieces)


def per_device(three_centre, pair_blocks, green_occ, occ_mask, green_virt, virt_mask, owner):
    z = lax.axis_index("grp")
    sub = lax.axis_index("sub")
    x, y, c = sub // 8, (sub // 2) % 4, sub % 2
    q1, q2 = jnp.where(c == 0, x, y), jnp.where(c == 0, y, x)

    def by_core(mine, other):
        return jnp.where(c == 0, jnp.stack([mine, other]), jnp.stack([other, mine]))

    go = green_occ * occ_mask[0, 0].astype(BF)
    go = by_core(
        lax.dynamic_slice_in_dim(go, c * 128, 128, 0),
        move(lax.dynamic_slice_in_dim(go, (1 - c) * 128, 128, 0), CORE),
    )
    go, theirs = tie(go, three_centre)
    t_oth = move(theirs, CORE)

    go1, go3, go2 = [move(go, FIRST[d]) for d in (1, 3, 2)]
    near = jnp.concatenate([go, go1, go2, go3])
    near, gv = tie(near, green_virt * virt_mask[0, 0].astype(BF))
    gv1, gv3, gv2 = [move(gv, DEPTH[r]) for r in (1, 3, 2)]
    set1, set3, set2 = [move(near, SECOND[e]) for e in (1, 3, 2)]
    gv = gv.reshape(1, 256, 256)
    strips = jnp.stack(
        [
            jnp.where(c == 0, s1 * 4 + s2, s2 * 4 + s1)
            for s1 in [(q1 + d) % 4 for d in (1, 2, 3, 0)]
            for s2 in [(q2 + e) % 4 for e in range(4)]
        ]
    ).astype(jnp.int32)
    gv = order_rows(strips, gv, move(gv, CORE))

    partners = by_core(pair_blocks[0], move(pair_blocks, CORE)[0]).reshape(4)
    places = jnp.concatenate([jnp.stack([c, q1, q2]), partners]).astype(jnp.int32)
    places, gv, set1, set3, set2 = tie(places, gv, set1, set3, set2)
    picked = pick(places, near, set1, set2, set3)
    gv1, gv3, gv2, picked = tie(gv1, gv3, gv2, picked)
    gv_rest = jnp.stack([gv1, gv3, gv2])
    gv_rest = order_rows(strips, gv_rest, move(gv_rest, CORE))
    far, *side = [move(picked, DEPTH[r]) for r in (2, 3, 1)]

    core = c.reshape(1).astype(jnp.int32)
    given = (core, *keep_half(core, three_centre, t_oth))
    sends0 = products_of(*given, gv, (picked, move(picked, CORE)), 1, 0, 0)
    *sends0, side3, side1 = tie(*sends0, *side)
    got0 = [move(sends0[d - 1], FIRST[d]) for d in (2, 1, 3)]
    halves = [h for a in (side1, side3) for h in (a, move(a, CORE))]
    sends1 = products_of(*given, gv_rest, halves, 2, 0, 0)
    *sends1, far = tie(*sends1, far)
    *got0, far = tie(*got0, far)
    sends2 = products_of(*given, gv_rest, (far, move(far, CORE)), 1, 0, 2)

    def sum_of(sends, got):
        total = sends[3]
        for part in got:
            total = total + part.astype(F32)
        return total

    got1 = [move(sends1[d - 1], FIRST[d]) for d in (2, 1, 3)]
    got2 = [move(sends2[d - 1], FIRST[d]) for d in (2, 1, 3)]
    sums = [sum_of(sends0, got0), sum_of(sends1, got1), sum_of(sends2, got2)]

    def strip(e):
        return jnp.concatenate([t[:, :, e * 16 : (e + 1) * 16] for t in sums])

    parts = [t[n] for t in sums for n in range(t.shape[0])]
    arrived = [move(strip(e).astype(BF), SECOND[e]) for e in (2, 1, 3)]

    def total(group):
        added = parts[group][:, 0:16]
        for part in arrived:
            added = added + part[group].astype(F32)
        return added.astype(BF)

    rows = jnp.stack(
        [total(0)] + [move(total(at), DEPTH[4 - r]) for at, r in ((3, 2), (1, 1), (2, 3))]
    )
    mine = lax.dynamic_slice_in_dim(rows, c * 128, 128, 3)
    other = move(lax.dynamic_slice_in_dim(rows, (1 - c) * 128, 128, 3), CORE)
    pieces = jnp.concatenate(
        [mine.reshape(32, 16, 128), other.reshape(32, 16, 128), jnp.zeros((1, 16, 128), BF)]
    )

    owner_flat = owner[:, 0]
    slab = owner_flat.shape[0]
    numbers = jnp.arange(slab, dtype=jnp.int32)
    earlier = (owner_flat[None, :] == owner_flat[:, None]) & (numbers[None, :] < numbers[:, None])
    position = jnp.sum(earlier.astype(jnp.int32), axis=1)
    slots = owner_flat * CAP + position
    distance = (numbers // 16 - z + 4) % 4
    stands = (distance % 2) * 2 + distance // 2
    at = jnp.where((numbers // 8) % 2 == c, 0, 32) + stands * 8 + numbers % 8
    match = slots[None, :] == jnp.arange(32 * CAP, dtype=jnp.int32)[:, None]
    source = jnp.min(jnp.where(match, at[None, :], 64), axis=1)
    outgoing = fill_slots(source, pieces)
    arrived = lax.all_to_all(
        outgoing.reshape(32, CAP, 16, 128), "sub", split_axis=0, concat_axis=0, tiled=True
    )
    return widen(arrived).reshape(1, CAP, 256, 256)


def solution(mesh):
    in_specs = (
        P("grp", "sub", None),
        P("sub", None),
        P("sub", "grp"),
        P("sub", "grp"),
        P("grp", "sub"),
        P("grp", "sub"),
        P(),
    )
    out_specs = P("grp", "sub", None, None)
    return jax.shard_map(
        per_device, mesh=mesh, in_specs=in_specs, out_specs=out_specs, check_vma=False
    )
```

```python
import jax
import jax.numpy as jnp
from jax import lax
from jax.experimental import pallas as pl
from jax.experimental.pallas import tpu as pltpu
from jax.sharding import PartitionSpec as P

CAP = 3
AXES = ("grp", "sub")
BF = jnp.bfloat16
F32 = jnp.float32
MIB = 1024 * 1024
STACK = 4


def pairs(target):
    out = []
    for z in range(4):
        for x in range(4):
            for y in range(4):
                for c in range(2):
                    tz, tx, ty, tc = target(z, x, y, c)
                    to = (tz % 4) * 32 + ((tx % 4) * 4 + ty % 4) * 2 + tc
                    out.append((z * 32 + (x * 4 + y) * 2 + c, to))
    return out


def along(number, d):
    def target(z, x, y, c):
        return (z, x + d, y, c) if c == number else (z, x, y + d, c)

    return pairs(target)


CORE = pairs(lambda z, x, y, c: (z, x, y, 1 - c))
FIRST = [along(0, d) for d in range(4)]
SECOND = [along(1, d) for d in range(4)]
DEPTH = [pairs(lambda z, x, y, c, d=d: (z + d, x, y, c)) for d in range(4)]


def move(value, permutation):
    return lax.ppermute(value, AXES, permutation)


def tie(*values):
    return lax.optimization_barrier(values)


def whole(shape):
    return pl.BlockSpec(shape, lambda *_: (0,) * len(shape))


def pick_body(sc, set0, set1, set2, set3, out, sem):
    c = sc[0]
    for k in range(4):
        block = sc[3 + k]
        tx, ty, tc = block // 8, (block // 2) % 4, block % 2
        t1 = jnp.where(c == 0, tx, ty)
        t2 = jnp.where(c == 0, ty, tx)
        at = ((sc[1] - t1 + 4) % 4) * 2 + tc
        far = (sc[2] - t2 + 4) % 4
        for e, source in enumerate((set0, set1, set2, set3)):

            @pl.when(far == e)
            def _(source=source):
                pltpu.make_async_copy(source.at[at], out.at[k], sem.at[k]).start()

    for k in range(4):
        pltpu.make_async_copy(set0.at[0], out.at[k], sem.at[k]).wait()


def pick(scalars, *sets):
    return pl.pallas_call(
        pick_body,
        grid_spec=pltpu.PrefetchScalarGridSpec(
            num_scalar_prefetch=1,
            grid=(1,),
            in_specs=[pl.BlockSpec(memory_space=pl.ANY)] * 4,
            out_specs=whole((4, 128, 256)),
            scratch_shapes=[pltpu.SemaphoreType.DMA((4,))],
        ),
        out_shape=jax.ShapeDtypeStruct((4, 128, 256), BF),
        compiler_params=pltpu.CompilerParams(vmem_limit_bytes=4 * MIB),
        cost_estimate=pl.CostEstimate(flops=0, bytes_accessed=1000, transcendentals=0),
    )(scalars, *sets)


def order_body(sc, own, oth, out):
    for k in range(16):
        rows = pl.ds(pl.multiple_of(sc[k] * 16, 16), 16)
        to = slice(k * 16, (k + 1) * 16)
        for r in range(out.shape[0]):
            out[r, to, 0:256] = own[r, rows, :]
            out[r, to, 256:512] = oth[r, rows, :]


def order_rows(strips, own, oth):
    count = own.shape[0]
    return pl.pallas_call(
        order_body,
        grid_spec=pltpu.PrefetchScalarGridSpec(
            num_scalar_prefetch=1,
            grid=(1,),
            in_specs=[whole((count, 256, 256))] * 2,
            out_specs=whole((count, 256, 512)),
        ),
        out_shape=jax.ShapeDtypeStruct((count, 256, 512), BF),
        compiler_params=pltpu.CompilerParams(vmem_limit_bytes=8 * MIB),
        cost_estimate=pl.CostEstimate(flops=0, bytes_accessed=1000, transcendentals=0),
    )(strips, own, oth)


def keep_half_body(sc, own, oth, out_own, out_oth, sem):
    rows = pl.ds(sc[0] * 8, 8)
    copies = [
        pltpu.make_async_copy(own.at[rows], out_own, sem.at[0]),
        pltpu.make_async_copy(oth.at[rows], out_oth, sem.at[1]),
    ]
    for copy in copies:
        copy.start()
    for copy in copies:
        copy.wait()


def keep_half(core, own, oth):
    shape = jax.ShapeDtypeStruct((8, 256, 512), BF)
    return pl.pallas_call(
        keep_half_body,
        in_specs=[pl.BlockSpec(memory_space=pltpu.SMEM)] + [pl.BlockSpec(memory_space=pl.ANY)] * 2,
        out_specs=[pl.BlockSpec(memory_space=pltpu.VMEM)] * 2,
        scratch_shapes=[pltpu.SemaphoreType.DMA((2,))],
        out_shape=[shape, shape],
        compiler_params=pltpu.CompilerParams(vmem_limit_bytes=10 * MIB),
        cost_estimate=pl.CostEstimate(flops=0, bytes_accessed=1000, transcendentals=0),
    )(core, *[pltpu.with_memory_space_constraint(t, pltpu.HBM) for t in (own, oth)])


def products_body(sc, t_own, t_oth, gv, *refs):
    halves, (send1, send2, send3, keep, go) = refs[: 2 * gv.shape[0]], refs[-5:]
    count = len(halves) // 2
    c = sc[0]

    @pl.when(pl.program_id(0) == 0)
    def _():
        for r in range(count):
            for n, half in enumerate((c, 1 - c)):
                for k in range(4):
                    rows = pl.ds(pl.multiple_of((k % 2) * 256 + half * 128, 128), 128)
                    go[2 * r + k // 2, rows, :] = halves[2 * r + n][k]

    for r in range(count):
        half_own = jnp.dot(
            t_own[...].reshape(STACK * 256, 512), go[2 * r + c], preferred_element_type=F32
        ).astype(BF)
        half_oth = jnp.dot(
            t_oth[...].reshape(STACK * 256, 512), go[2 * r + 1 - c], preferred_element_type=F32
        ).astype(BF)
        for p in range(STACK):
            rows = slice(p * 256, (p + 1) * 256)
            out = jnp.dot(gv[r, :, 0:256], half_own[rows], preferred_element_type=F32)
            out += jnp.dot(gv[r, :, 256:512], half_oth[rows], preferred_element_type=F32)
            send1[r, p] = out[0:64].astype(BF)
            send2[r, p] = out[64:128].astype(BF)
            send3[r, p] = out[128:192].astype(BF)
            keep[r, p] = out[192:256]


def products_of(core, t_own, t_oth, gv, halves, room, at, gv_at, begun=()):
    count = len(halves) // 2
    block = pl.BlockSpec((count, STACK, 64, 256), lambda p, sc: (at, p, 0, 0))
    shape = (room, 8, 64, 256)
    first = 4 + 2 * count
    functions = pl.BlockSpec((STACK, 256, 512), lambda p, sc: (p, 0, 0))
    return pl.pallas_call(
        products_body,
        grid_spec=pltpu.PrefetchScalarGridSpec(
            num_scalar_prefetch=1,
            grid=(8 // STACK,),
            in_specs=[functions] * 2
            + [pl.BlockSpec((count, 256, 512), lambda p, sc: (gv_at, 0, 0))]
            + [whole((4, 128, 256))] * (2 * count)
            + [pl.BlockSpec(memory_space=pl.ANY)] * len(begun),
            out_specs=[block] * 4,
            scratch_shapes=[pltpu.VMEM((2 * count, 512, 256), BF)],
        ),
        out_shape=[jax.ShapeDtypeStruct(shape, BF)] * 3 + [jax.ShapeDtypeStruct(shape, F32)],
        input_output_aliases={first + n: n for n in range(len(begun))},
        compiler_params=pltpu.CompilerParams(vmem_limit_bytes=(12 + 4 * count) * MIB),
        cost_estimate=pl.CostEstimate(flops=1000, bytes_accessed=1000, transcendentals=0),
    )(core, t_own, t_oth, gv, *halves, *begun)


def slots_body(sc, pieces, out):
    for s in range(32 * CAP):
        out[s] = pieces[sc[s]]


def fill_slots(source, pieces):
    return pl.pallas_call(
        slots_body,
        grid_spec=pltpu.PrefetchScalarGridSpec(
            num_scalar_prefetch=1,
            grid=(1,),
            in_specs=[whole((65, 16, 128))],
            out_specs=whole((32 * CAP, 16, 128)),
        ),
        out_shape=jax.ShapeDtypeStruct((32 * CAP, 16, 128), BF),
        compiler_params=pltpu.CompilerParams(vmem_limit_bytes=4 * MIB),
    )(source, pieces)


def widen_body(pieces, out):
    for n in range(32):
        rows, columns = slice(n // 2 * 16, n // 2 * 16 + 16), slice(n % 2 * 128, n % 2 * 128 + 128)
        for k in range(CAP):
            out[k, rows, columns] = pieces[n, k].astype(F32)


def widen(pieces):
    return pl.pallas_call(
        widen_body,
        in_specs=[pl.BlockSpec(memory_space=pltpu.VMEM)],
        out_specs=pl.BlockSpec(memory_space=pltpu.VMEM),
        out_shape=jax.ShapeDtypeStruct((CAP, 256, 256), F32),
        compiler_params=pltpu.CompilerParams(vmem_limit_bytes=8 * MIB),
    )(pieces)


def per_device(three_centre, pair_blocks, green_occ, occ_mask, green_virt, virt_mask, owner):
    z = lax.axis_index("grp")
    sub = lax.axis_index("sub")
    x, y, c = sub // 8, (sub // 2) % 4, sub % 2
    q1, q2 = jnp.where(c == 0, x, y), jnp.where(c == 0, y, x)

    def by_core(mine, other):
        return jnp.where(c == 0, jnp.stack([mine, other]), jnp.stack([other, mine]))

    go = green_occ * occ_mask[0, 0].astype(BF)
    go = by_core(
        lax.dynamic_slice_in_dim(go, c * 128, 128, 0),
        move(lax.dynamic_slice_in_dim(go, (1 - c) * 128, 128, 0), CORE),
    )
    go, theirs, pair_oth = tie(go, three_centre, move(pair_blocks, CORE))
    t_oth = move(theirs, CORE)

    go1, go3, go2 = [move(go, FIRST[d]) for d in (1, 3, 2)]
    near = jnp.concatenate([go, go1, go2, go3])
    near, gv = tie(near, green_virt * virt_mask[0, 0].astype(BF))
    gv1, gv3, gv2 = [move(gv, DEPTH[r]) for r in (1, 3, 2)]
    set1, set3, set2 = [move(near, SECOND[e]) for e in (1, 3, 2)]
    gv = gv.reshape(1, 256, 256)
    strips = jnp.stack(
        [
            jnp.where(c == 0, s1 * 4 + s2, s2 * 4 + s1)
            for s1 in [(q1 + d) % 4 for d in (1, 2, 3, 0)]
            for s2 in [(q2 + e) % 4 for e in range(4)]
        ]
    ).astype(jnp.int32)
    gv = order_rows(strips, gv, move(gv, CORE))

    partners = by_core(pair_blocks[0], pair_oth[0]).reshape(4)
    places = jnp.concatenate([jnp.stack([c, q1, q2]), partners]).astype(jnp.int32)
    places, gv, set1, set3, set2 = tie(places, gv, set1, set3, set2)
    picked = pick(places, near, set1, set2, set3)
    gv1, gv3, gv2, picked = tie(gv1, gv3, gv2, picked)
    gv_rest = jnp.stack([gv1, gv3, gv2])
    gv_rest = order_rows(strips, gv_rest, move(gv_rest, CORE))
    far, *side = [move(picked, DEPTH[r]) for r in (2, 3, 1)]

    core = c.reshape(1).astype(jnp.int32)
    given = (core, *keep_half(core, three_centre, t_oth))
    sends0 = products_of(*given, gv, (picked, move(picked, CORE)), 1, 0, 0)
    *_, side3, side1 = tie(*sends0, *side)
    got0 = [move(sends0[d - 1], FIRST[d]) for d in (2, 1, 3)]
    halves = [h for a in (side1, side3) for h in (a, move(a, CORE))]
    sends1 = products_of(*given, gv_rest, halves, 2, 0, 0)
    *_, far = tie(*sends1, far)
    *got0, far = tie(*got0, far)
    sends2 = products_of(*given, gv_rest, (far, move(far, CORE)), 1, 0, 2)

    def sum_of(sends, got):
        total = sends[3]
        for part in got:
            total = total + part.astype(F32)
        return total

    got1 = [move(sends1[d - 1], FIRST[d]) for d in (2, 1, 3)]
    got2 = [move(sends2[d - 1], FIRST[d]) for d in (2, 1, 3)]
    sums = [sum_of(sends0, got0), sum_of(sends1, got1), sum_of(sends2, got2)]

    def strip(e):
        return jnp.concatenate([t[:, :, e * 16 : (e + 1) * 16] for t in sums])

    total = strip(0)
    for e in (2, 1, 3):
        total = total + move(strip(e).astype(BF), SECOND[e]).astype(F32)
    total = total.astype(BF)

    rows = jnp.stack(
        [total[0]] + [move(total[at], DEPTH[4 - r]) for at, r in ((3, 2), (1, 1), (2, 3))]
    )
    mine = lax.dynamic_slice_in_dim(rows, c * 128, 128, 3)
    other = move(lax.dynamic_slice_in_dim(rows, (1 - c) * 128, 128, 3), CORE)
    pieces = jnp.concatenate(
        [mine.reshape(32, 16, 128), other.reshape(32, 16, 128), jnp.zeros((1, 16, 128), BF)]
    )

    owner_flat = owner[:, 0]
    slab = owner_flat.shape[0]
    numbers = jnp.arange(slab, dtype=jnp.int32)
    earlier = (owner_flat[None, :] == owner_flat[:, None]) & (numbers[None, :] < numbers[:, None])
    position = jnp.sum(earlier.astype(jnp.int32), axis=1)
    slots = owner_flat * CAP + position
    distance = (numbers // 16 - z + 4) % 4
    stands = (distance % 2) * 2 + distance // 2
    at = jnp.where((numbers // 8) % 2 == c, 0, 32) + stands * 8 + numbers % 8
    match = slots[None, :] == jnp.arange(32 * CAP, dtype=jnp.int32)[:, None]
    source = jnp.min(jnp.where(match, at[None, :], 64), axis=1)
    outgoing = fill_slots(source, pieces)
    arrived = lax.all_to_all(
        outgoing.reshape(32, CAP, 16, 128), "sub", split_axis=0, concat_axis=0, tiled=True
    )
    return widen(arrived).reshape(1, CAP, 256, 256)


def solution(mesh):
    in_specs = (
        P("grp", "sub", None),
        P("sub", None),
        P("sub", "grp"),
        P("sub", "grp"),
        P("grp", "sub"),
        P("grp", "sub"),
        P(),
    )
    out_specs = P("grp", "sub", None, None)
    return jax.shard_map(
        per_device, mesh=mesh, in_specs=in_specs, out_specs=out_specs, check_vma=False
    )
```
